256 devices in a mesh: ctx: 32 (over z, y_hi, core), kvh: 8 (over y_lo, x).
Axes of the slice: x: 4, y: 4 (y_hi: 2, y_lo: 2; y = y_hi * 2 + y_lo), z: 8, core: 2. Of those that a mesh axis runs over, the one named last changes fastest.
Arguments:
- queries: bfloat16 [2, 4096, 5120], P(None, 'ctx', 'kvh'), may hold values from -140 to 140
- keys: bfloat16 [4096, 1024], P('ctx', 'kvh'), may hold values from -8 to 8
- values: bfloat16 [4096, 1024], P('ctx', 'kvh'), may hold values from -6 to 6
- grad_out: bfloat16 [2, 4096, 5120], P(None, 'ctx', 'kvh'), may hold values from -6 to 6
- query_weight: bfloat16 [2, 5120, 5120], P(None, 'ctx', 'kvh'), may hold values from -0.078125 to 0.078125
Outputs:
- input_grads: bfloat16 [2, 4096, 5120], P(None, 'ctx', 'kvh')
- grad_keys: bfloat16 [4096, 1024], P('ctx', 'kvh')
- grad_values: bfloat16 [4096, 1024], P('ctx', 'kvh')
The draws below stay inside these ranges and needn't reach their ends.
All inputs are finite; a program needn't handle non-finite values.
Results may differ from the reference program's by a relative error of at most 0.0058.
Values may be sent and summed in bfloat16 or wider, within the bound.
A program may use at most 128 MiB of HBM per device.

```python
import jax
import jax.numpy as jnp
from jax import lax

D = 5120
HEADS = 40
KV_HEADS = 8
HEAD_DIM = 128
LAYERS = 2
TOKENS = 4096


def shared_keys(key):
    return jnp.clip(jax.random.normal(key, (TOKENS, KV_HEADS * HEAD_DIM), jnp.float32), -6.0, 6.0)


def draw_keys(key, part):
    shared = shared_keys(key)
    return shared.astype(jnp.bfloat16)


def draw_queries(key, part):
    key = jax.random.fold_in(key, 23)
    fresh = jnp.clip(jax.random.normal(key, (LAYERS, TOKENS, HEADS * HEAD_DIM), jnp.float32), -6.0, 6.0)
    return fresh.astype(jnp.bfloat16)


def block_levels(stream_key, extent, split, least, largest):
    gain = 1.0
    for dim, blocks in split:
        steps = jax.random.uniform(jax.random.fold_in(jax.random.fold_in(stream_key, 6), dim), (blocks,), jnp.float32, least / len(split), largest / len(split))
        gain = gain * jnp.repeat(jnp.exp(steps), extent[dim] // blocks).reshape((-1,) + (1,) * (len(extent) - 1 - dim))
    return gain


def normal_values(own_key, extent, width, reach, pieces=(), kind=jnp.bfloat16):
    factor_of = block_levels(own_key, extent, pieces, -0.22, 0.18) if pieces else 1.0
    array = jax.random.normal(own_key, extent, jnp.float32) * width * factor_of
    return jnp.minimum(jnp.maximum(array, -reach), reach).astype(kind)


def setup_inputs(seed: int = 0) -> dict:
    seeds = jax.random.split(jax.random.key(seed), 6)
    return {
        "queries": draw_queries(jax.random.fold_in(seeds[5], 71), 0),
        "keys": draw_keys(jax.random.fold_in(seeds[5], 71), 0),
        "values": normal_values(seeds[2], (TOKENS, KV_HEADS * HEAD_DIM), 1.0, 6.0, ((0, 32), (1, 8))),
        "grad_out": normal_values(seeds[3], (LAYERS, TOKENS, HEADS * HEAD_DIM), 1.0, 6.0, ((1, 32), (2, 8))),
        "query_weight": normal_values(seeds[4], (LAYERS, D, HEADS * HEAD_DIM), (HEADS * HEAD_DIM) ** -0.5, 0.078125, ((1, 32), (2, 8))),
    }


lowest = -1.0e30


def reference(queries, keys, values, grad_out, query_weight):
    scale_factor = HEAD_DIM ** -0.5
    repeat = HEADS // KV_HEADS
    positions = jnp.arange(TOKENS, dtype=jnp.int32)
    causal = positions[None, :] <= positions[:, None]

    def one_head(carry_state, index):
        key_sums, value_sums = carry_state
        layer_idx = index // HEADS
        head_idx = index % HEADS
        group_col = (head_idx // repeat) * HEAD_DIM
        head_col = head_idx * HEAD_DIM
        query = lax.dynamic_slice_in_dim(queries[layer_idx], head_col, HEAD_DIM, 1).astype(jnp.float32)
        cotangent = lax.dynamic_slice_in_dim(grad_out[layer_idx], head_col, HEAD_DIM, 1).astype(jnp.float32)
        key_cols = lax.dynamic_slice_in_dim(keys, group_col, HEAD_DIM, 1).astype(jnp.float32)
        value_cols = lax.dynamic_slice_in_dim(values, group_col, HEAD_DIM, 1).astype(jnp.float32)
        scores = jnp.dot(query, key_cols.T, precision=lax.Precision.HIGHEST) * scale_factor
        scores = jnp.where(causal, scores, lowest)
        peak = jnp.max(scores, axis=1, keepdims=True)
        expd = jnp.where(causal, jnp.exp(scores - peak), 0.0)
        probs = expd / jnp.sum(expd, axis=1, keepdims=True)
        slopes = jnp.dot(cotangent, value_cols.T, precision=lax.Precision.HIGHEST)
        centre = jnp.sum(probs * slopes, axis=1, keepdims=True)
        mixed = lax.optimization_barrier((probs * (slopes - centre)).astype(jnp.bfloat16)).astype(jnp.float32)
        rounded = lax.optimization_barrier(probs.astype(jnp.bfloat16)).astype(jnp.float32)
        query_grad = jnp.dot(mixed, key_cols, precision=lax.Precision.HIGHEST) * scale_factor
        key_grad = jnp.dot(mixed.T, query, precision=lax.Precision.HIGHEST) * scale_factor
        value_grad = jnp.dot(rounded.T, cotangent, precision=lax.Precision.HIGHEST)
        key_sums = lax.dynamic_update_slice_in_dim(key_sums, lax.dynamic_slice_in_dim(key_sums, group_col, HEAD_DIM, 1) + key_grad, group_col, 1)
        value_sums = lax.dynamic_update_slice_in_dim(value_sums, lax.dynamic_slice_in_dim(value_sums, group_col, HEAD_DIM, 1) + value_grad, group_col, 1)
        return (key_sums, value_sums), query_grad.astype(jnp.bfloat16)

    start_state = (jnp.zeros((TOKENS, KV_HEADS * HEAD_DIM), jnp.float32), jnp.zeros((TOKENS, KV_HEADS * HEAD_DIM), jnp.float32))
    (key_sums, value_sums), per_head = lax.scan(one_head, start_state, jnp.arange(LAYERS * HEADS, dtype=jnp.int32))
    grad_queries = per_head.reshape(LAYERS, HEADS, TOKENS, HEAD_DIM).transpose(0, 2, 1, 3).reshape(LAYERS, TOKENS, HEADS * HEAD_DIM)
    layer_grads = []
    for layer_idx in range(LAYERS):
        layer_grads.append(jnp.dot(grad_queries[layer_idx].astype(jnp.float32), query_weight[layer_idx].astype(jnp.float32).T, precision=lax.Precision.HIGHEST))
    input_grads = jnp.stack(layer_grads).astype(jnp.bfloat16)
    return input_grads, key_sums.astype(jnp.bfloat16), value_sums.astype(jnp.bfloat16)
```

```python
import jax
import jax.numpy as jnp
from jax import lax
from jax.experimental import pallas as pl
from jax.experimental.pallas import tpu as pltpu
from jax.sharding import PartitionSpec as P

SCALE = 128 ** -0.5
LOG2 = SCALE * 1.4426950408889634
LOWEST = -1e30
NT = (((1,), (1,)), ((), ()))
MESH = pl.DeviceIdType.MESH
BF = jnp.bfloat16
F32 = jnp.float32
BLOCK = 2048
SUB = 128
PARTS = BLOCK // SUB
PAIRS = 5
POLLS = 14


def dot_nt(a, b):
    return lax.dot_general(a, b, NT, preferred_element_type=F32)


def dot(a, b):
    return jnp.dot(a, b, preferred_element_type=F32)


def send(src, dst, send_sem, recv_sem, device):
    return pltpu.make_async_remote_copy(
        src_ref=src,
        dst_ref=dst,
        send_sem=send_sem,
        recv_sem=recv_sem,
        device_id=device,
        device_id_type=MESH,
    )


def kernel(
    q_ref, k_ref, v_ref, do_ref, w_ref,
    out_ref, gk_ref, gv_ref,
    kv, kt, e_ref, d_ref, peaks, qs, dos, dkv, w_all, a_all, ct, xr, fs, fr,
    sb, sbr, yb, ybr, zb, zr,
    kv_y, kv_rs, kv_rr, kv_ls, kv_lr, kv_ss, kv_sr,
    w_y, w_rs, w_rr, w_ls, w_lr, w_ss, w_sr,
    a_s, a_r, x_s, x_r, f_s, f_r,
    s_s, s_r, y_s, y_r, z_s, z_r,
):
    i = lax.axis_index("ctx")
    j = lax.axis_index("kvh")
    z = lax.div(i, 4)
    r = lax.rem(i, 4)
    yh = lax.div(r, 2)
    c = lax.rem(i, 2)
    yl = lax.div(j, 4)
    x = lax.rem(j, 4)

    def ring(a):
        return lax.rem(a + 8, 8)

    sibling = {"ctx": i + 1 - 2 * c, "kvh": j}
    right = {"ctx": ring(z + 1) * 4 + r, "kvh": j}
    left = {"ctx": ring(z - 1) * 4 + r, "kvh": j}
    flip_i = i + 2 - 4 * yh
    flip_j = j + 4 - 8 * yl
    y_peers = [{"ctx": flip_i, "kvh": j}, {"ctx": i, "kvh": flip_j}, {"ctx": flip_i, "kvh": flip_j}]
    y_places = [(1 - yh, yl), (yh, 1 - yl), (1 - yh, 1 - yl)]
    x_places = [lax.rem(x + t, 4) for t in (1, 2, 3)]
    x_peers = [{"ctx": i, "kvh": yl * 4 + p} for p in x_places]

    barrier = pltpu.get_barrier_semaphore()
    for peer in [sibling] + y_peers + x_peers:
        pl.semaphore_signal(barrier, inc=1, device_id=peer, device_id_type=MESH)
    for t in range(1, 8):
        pl.semaphore_signal(
            barrier, inc=1, device_id={"ctx": ring(z + t) * 4 + r, "kvh": j}, device_id_type=MESH
        )
    pl.semaphore_wait(barrier, 14)

    kv[0, z, yh, c] = k_ref[...]
    kv[1, z, yh, c] = v_ref[...]
    own = kv.at[:, z, yh, c]
    kv_far = send(own, own, kv_y.at[0], kv_y.at[1], y_peers[0])
    kv_far.start()
    sib_sends = []

    def to_sibling(ref):
        n = len(sib_sends)
        copy = send(ref, ref, kv_ss.at[n], kv_sr.at[n], sibling)
        copy.start()
        sib_sends.append(copy)

    to_sibling(own)
    w_swap = send(
        w_ref.at[:, pl.ds(pl.multiple_of((1 - yl) * 80, 16), 80), :],
        w_all.at[:, yl, z, c],
        w_y.at[0],
        w_y.at[1],
        y_peers[1],
    )
    w_swap.start()
    w_all[:, yl, z, c] = w_ref[:, pl.ds(pl.multiple_of(yl * 80, 16), 80), :]
    kv_far.wait_recv()
    block = kv.at[:, z, :, c]
    rights = [send(block, block, kv_rs.at[0], kv_rr.at[0], right)]
    lefts = [send(block, block, kv_ls.at[0], kv_lr.at[0], left)]
    rights[0].start()
    lefts[0].start()
    to_sibling(kv.at[:, z, 1 - yh, c])
    dkv[...] = jnp.zeros_like(dkv)
    for s in range(4):
        for sends, toward, ss, rs, sign, half in (
            (rights, right, kv_rs, kv_rr, -1, 0),
            (lefts, left, kv_ls, kv_lr, 1, 1),
        ):
            sends[s].wait_recv()
            zz = ring(z + sign * (s + 1))
            block = kv.at[:, zz, :, c] if s < 3 else kv.at[half, zz, :, c]
            if s < 3:
                onward = block if s < 2 else kv.at[half, zz, :, c]
                copy = send(onward, onward, ss.at[s + 1], rs.at[s + 1], toward)
                copy.start()
                sends.append(copy)
            to_sibling(block)

    def w_part(layer, half, zz):
        return w_all.at[layer, half, zz, c]

    def w_send(layer, half, zz, n):
        ref = w_part(layer, half, zz)
        if layer == 0:
            return send(ref, ref, w_rs.at[n], w_rr.at[n], right)
        return send(ref, ref, w_ls.at[n], w_lr.at[n], left)

    def w_sib(layer, half, zz, n):
        ref = w_part(layer, half, zz)
        return send(ref, ref, w_ss.at[layer, n], w_sr.at[layer, n], sibling)

    w_swap.wait_recv()
    for half in range(2):
        for layer in range(2):
            w_send(layer, half, z, half).start()
    for half in range(2):
        for layer in range(2):
            w_sib(layer, half, z, half).start()

    def poll(n):
        step = lax.div(n, 2)
        half = lax.rem(n, 2)
        for layer, sign in ((0, -1), (1, 1)):
            zz = ring(z + sign * (step + 1))
            w_send(layer, half, zz, n).wait_recv()

            @pl.when(step < 6)
            def _():
                w_send(layer, half, zz, n + 2).start()

            w_sib(layer, half, zz, n + 2).start()

    for copy in sib_sends:
        copy.wait_recv()

    for b in range(8):
        whole = kv[0, b].reshape(512, 128).astype(F32)
        kt[b // 4, :, (b % 4) * 512 : (b % 4 + 1) * 512] = whole.T.astype(BF)

    last = lax.div(z, 4)
    lane = lax.broadcasted_iota(jnp.int32, (SUB, 256), 1)
    place = z * 512 + r * 128 + lax.rem(lane, 128)

    def pair(h, carry):
        column = pl.ds(pl.multiple_of(h * 128, 128), 128)
        for layer in range(2):
            rows = slice(layer * 128, (layer + 1) * 128)
            qs[rows] = q_ref[layer, :, column]
            dos[rows] = do_ref[layer, :, column]
        query = qs[...]
        cotangent = dos[...]

        def forward(b, state, masked=False):
            m, total, weighted = state
            for n in range(PARTS):
                rows = pl.ds(n * SUB, SUB)
                zz = 4 * b + n // 4
                s = dot_nt(kv[0, zz, n // 2 % 2, n % 2], query)
                if masked:
                    key_place = lax.broadcasted_iota(jnp.int32, (SUB, 256), 0) + (b * BLOCK + n * SUB)
                    s = jnp.where(key_place <= place, s, LOWEST)
                d = dot_nt(kv[1, zz, n // 2 % 2, n % 2], cotangent)
                s = s.reshape(SUB // 8, 8, 256)
                peak = jnp.max(s, axis=0)
                e = jnp.exp2((s - peak[None]) * LOG2)
                part_total = jnp.sum(e, axis=0)
                part_weighted = jnp.sum(e * d.reshape(SUB // 8, 8, 256), axis=0)
                e_ref[b, rows] = e.reshape(SUB, 256)
                d_ref[b, rows] = d
                peaks[b, n] = peak
                new = jnp.maximum(m, peak)
                f0 = jnp.exp2((m - new) * LOG2)
                f1 = jnp.exp2((peak - new) * LOG2)
                total = total * f0 + part_total * f1
                weighted = weighted * f0 + part_weighted * f1
                m = new
            return m, total, weighted

        zero = jnp.zeros((8, 256), F32)
        state = lax.fori_loop(0, last, forward, (jnp.full((8, 256), LOWEST, F32), zero, zero))
        m8, total8, weighted8 = forward(last, state, True)
        poll(2 * h)
        m = jnp.max(m8, axis=0, keepdims=True)
        f = jnp.exp2((m8 - m) * LOG2)
        inverse = 1.0 / jnp.sum(total8 * f, axis=0, keepdims=True)
        delta = jnp.sum(weighted8 * f, axis=0, keepdims=True) * inverse

        def backward(b, dq):
            probs = []
            mixed = []
            for n in range(PARTS):
                rows = pl.ds(n * SUB, SUB)
                f = jnp.exp2((peaks[b, n] - m) * LOG2) * inverse
                p = (e_ref[b, rows].reshape(SUB // 8, 8, 256) * f[None]).reshape(SUB, 256)
                mixed.append((p * (d_ref[b, rows] - delta)).astype(BF))
                probs.append(p.astype(BF))
            probs = jnp.concatenate(probs, 0)
            mixed = jnp.concatenate(mixed, 0)
            here = pl.ds(4 * b, 4)
            shape = (4, 2, 2, 128, 128)
            dkv[1, here] += dot(probs, cotangent).reshape(shape)
            dkv[0, here] += dot(mixed, query).reshape(shape)
            return dq + dot(kt[b], mixed)

        dq = lax.fori_loop(0, last + 1, backward, jnp.zeros((128, 256), F32))
        for layer in range(2):
            a_all[h, layer, yl, yh] = (dq[:, layer * 128 : (layer + 1) * 128].T * SCALE).astype(BF)
        ref = a_all.at[h, :, yl, yh]
        for t in range(3):
            send(ref, ref, a_s.at[h, t], a_r.at[h, t], y_peers[t]).start()
        poll(2 * h + 1)
        return carry

    lax.fori_loop(0, PAIRS, pair, 0)

    def stage_sibling(zz, carry):
        sb[0, zz] = (dkv[0, zz, :, 1 - c] * SCALE).astype(BF)
        sb[1, zz] = dkv[1, zz, :, 1 - c].astype(BF)
        send(sb.at[:, zz], sbr.at[:, zz], s_s.at[zz], s_r.at[zz], sibling).start()
        return carry

    lax.fori_loop(0, z + 1, stage_sibling, 0)

    def late(n, carry):
        poll(n)
        return carry

    lax.fori_loop(2 * PAIRS, POLLS, late, 0)

    def stage_y(zz, carry):
        copy = send(sb.at[:, zz], sbr.at[:, zz], s_s.at[zz], s_r.at[zz], sibling)
        copy.wait_recv()
        for n, scale in ((0, SCALE), (1, 1.0)):
            far = dkv[n, zz, 1 - yh, c] * scale + sbr[n, zz, 1 - yh].astype(F32)
            yb[n, zz] = far.astype(BF)
        send(yb.at[:, zz], ybr.at[:, zz], y_s.at[zz], y_r.at[zz], y_peers[0]).start()
        for n, scale in ((0, SCALE), (1, 1.0)):
            dkv[n, zz, yh, c] = dkv[n, zz, yh, c] * scale + sbr[n, zz, yh].astype(F32)
        return carry

    lax.fori_loop(0, z + 1, stage_y, 0)

    for h in range(PAIRS):
        for t, (ph, pw) in enumerate(y_places):
            ref = a_all.at[h, :, pw, ph]
            send(ref, ref, a_s.at[h, t], a_r.at[h, t], y_peers[t]).wait_recv()
    for layer in range(2):
        for n in range(16):
            zz = ring(z - n // 2) if layer == 0 else ring(z + n // 2)
            w_sib(layer, n % 2, zz, n).wait_recv()
    x_sends = []
    for layer in range(2):
        sides = [
            jnp.concatenate([a_all[h, layer, w].reshape(256, 128) for h in range(PAIRS)], axis=1)
            for w in range(2)
        ]
        for hi in range(2):
            total = dot_nt(w_all[layer, 0, 4 * hi : 4 * hi + 4].reshape(640, 640), sides[0])
            total = total + dot_nt(w_all[layer, 1, 4 * hi : 4 * hi + 4].reshape(640, 640), sides[1])
            ct[layer, hi] = total.astype(BF).reshape(4, 2, 80, 256)
        for t in range(3):
            copy = send(
                ct.at[layer, :, x_places[t]], xr.at[t, layer], x_s.at[layer, t], x_r.at[layer, t], x_peers[t]
            )
            copy.start()
            x_sends.append(copy)

    def stage_z(zz, carry):
        send(yb.at[:, zz], ybr.at[:, zz], y_s.at[zz], y_r.at[zz], y_peers[0]).wait_recv()
        for n in range(2):
            near = dkv[n, zz, yh, c] + ybr[n, zz].astype(F32)
            dkv[n, zz, yh, c] = near
            zb[n, zz] = near.astype(BF)

        @pl.when(zz < z)
        def _():
            send(
                zb.at[:, zz], zr.at[:, z], z_s.at[zz], z_r.at[z], {"ctx": zz * 4 + r, "kvh": j}
            ).start()

        return carry

    lax.fori_loop(0, z + 1, stage_z, 0)

    f_sends = []
    for layer in range(2):
        for t in range(3):
            x_sends[layer * 3 + t].wait_recv()
        total = ct[layer, :, x].astype(F32)
        for t in range(3):
            total = total + xr[t, layer].astype(F32)
        total = total.astype(BF)
        for half in range(2):
            fs[half, :, layer] = total[..., half * 128 : (half + 1) * 128]
        for t, (ph, pw) in enumerate(y_places):
            copy = send(
                fs.at[ph, pw, layer], fr.at[layer, yh, :, yl], f_s.at[layer, t], f_r.at[layer, t], y_peers[t]
            )
            copy.start()
            f_sends.append(copy)
        fr[layer, yh, :, yl] = fs[yh, yl, layer]

    def gather_z(zz, carry):
        send(zb.at[:, z], zr.at[:, zz], z_s.at[z], z_r.at[zz], left).wait_recv()
        for n in range(2):
            dkv[n, z, yh, c] += zr[n, zz].astype(F32)
        return carry

    lax.fori_loop(z + 1, 8, gather_z, 0)
    gk_ref[...] = dkv[0, z, yh, c].astype(BF)
    gv_ref[...] = dkv[1, z, yh, c].astype(BF)

    for layer in range(2):
        for t in range(3):
            f_sends[layer * 3 + t].wait_recv()
        out_ref[layer] = fr[layer].reshape(640, 128).astype(F32).T.astype(BF)

    for copy in [kv_far, w_swap] + sib_sends + rights + lefts + x_sends + f_sends:
        copy.wait_send()
    for n in range(POLLS):
        for layer in range(2):
            w_send(layer, 0, z, n).wait_send()
    for n in range(POLLS + 2):
        for layer in range(2):
            w_sib(layer, 0, z, n).wait_send()
    for h in range(PAIRS):
        for t in range(3):
            ref = a_all.at[h, :, yl, yh]
            send(ref, ref, a_s.at[h, t], a_r.at[h, t], y_peers[t]).wait_send()

    def drain(zz, carry):
        send(sb.at[:, zz], sbr.at[:, zz], s_s.at[zz], s_r.at[zz], sibling).wait_send()
        send(yb.at[:, zz], ybr.at[:, zz], y_s.at[zz], y_r.at[zz], y_peers[0]).wait_send()

        @pl.when(zz < z)
        def _():
            send(zb.at[:, zz], zr.at[:, z], z_s.at[zz], z_r.at[z], left).wait_send()

        return carry

    lax.fori_loop(0, z + 1, drain, 0)


def body(queries, keys, values, grad_out, query_weight):
    dma = pltpu.SemaphoreType.DMA
    vmem = pltpu.VMEM
    return pl.pallas_call(
        kernel,
        out_shape=(
            jax.ShapeDtypeStruct((2, 128, 640), BF),
            jax.ShapeDtypeStruct((128, 128), BF),
            jax.ShapeDtypeStruct((128, 128), BF),
        ),
        in_specs=[pl.BlockSpec(memory_space=pltpu.VMEM)] * 5,
        out_specs=[pl.BlockSpec(memory_space=pltpu.VMEM)] * 3,
        scratch_shapes=[
            vmem((2, 8, 2, 2, 128, 128), BF),
            vmem((2, 128, BLOCK), BF),
            vmem((2, BLOCK, 256), F32),
            vmem((2, BLOCK, 256), F32),
            vmem((2, PARTS, 8, 256), F32),
            vmem((256, 128), BF),
            vmem((256, 128), BF),
            vmem((2, 8, 2, 2, 128, 128), F32),
            vmem((2, 2, 8, 2, 80, 640), BF),
            vmem((PAIRS, 2, 2, 2, 128, 128), BF),
            vmem((2, 2, 4, 2, 80, 256), BF),
            vmem((3, 2, 2, 2, 80, 256), BF),
            vmem((2, 2, 2, 2, 80, 128), BF),
            vmem((2, 2, 2, 2, 80, 128), BF),
            vmem((2, 8, 2, 128, 128), BF),
            vmem((2, 8, 2, 128, 128), BF),
            vmem((2, 8, 128, 128), BF),
            vmem((2, 8, 128, 128), BF),
            vmem((2, 8, 128, 128), BF),
            vmem((2, 8, 128, 128), BF),
            dma((2,)), dma((4,)), dma((4,)), dma((4,)), dma((4,)), dma((10,)), dma((10,)),
            dma((2,)), dma((POLLS,)), dma((POLLS,)), dma((POLLS,)), dma((POLLS,)),
            dma((2, POLLS + 2)), dma((2, POLLS + 2)),
            dma((PAIRS, 3)), dma((PAIRS, 3)), dma((2, 3)), dma((2, 3)), dma((2, 3)), dma((2, 3)),
            dma((8,)), dma((8,)), dma((8,)), dma((8,)), dma((8,)), dma((8,)),
        ],
        compiler_params=pltpu.CompilerParams(
            collective_id=0, has_side_effects=True, vmem_limit_bytes=56 << 20
        ),
    )(queries, keys, values, grad_out, query_weight)


def solution(mesh):
    cols = P(None, "ctx", "kvh")
    flat = P("ctx", "kvh")
    return jax.shard_map(
        body,
        mesh=mesh,
        in_specs=(cols, flat, flat, cols, cols),
        out_specs=(cols, flat, flat),
        check_vma=False,
    )
```

```python
import jax
import jax.numpy as jnp
from jax import lax
from jax.experimental import pallas as pl
from jax.experimental.pallas import tpu as pltpu
from jax.sharding import PartitionSpec as P

SCALE = 128 ** -0.5
LOG2 = SCALE * 1.4426950408889634
LOWEST = -1e30
NT = (((1,), (1,)), ((), ()))
MESH = pl.DeviceIdType.MESH
BF = jnp.bfloat16
F32 = jnp.float32
BLOCK = 2048
SUB = 128
PARTS = BLOCK // SUB
PAIRS = 5


def dot_nt(a, b):
    return lax.dot_general(a, b, NT, preferred_element_type=F32)


def dot(a, b):
    return jnp.dot(a, b, preferred_element_type=F32)


def send(src, dst, send_sem, recv_sem, device):
    return pltpu.make_async_remote_copy(
        src_ref=src,
        dst_ref=dst,
        send_sem=send_sem,
        recv_sem=recv_sem,
        device_id=device,
        device_id_type=MESH,
    )


def kernel(
    q_ref, k_ref, v_ref, do_ref, w_ref,
    out_ref, gk_ref, gv_ref,
    kv, kt, e_ref, d_ref, peaks, qs, dos, dkv, w_all, a_all, ct, xr, fs, fr,
    sb, sbr, yb, ybr, zb, zr,
    kv_s, kv_r, ky_s, ky_r, kc_s, kc_r,
    ws_s, ws_r, w_s, w_r, wc_s, wc_r,
    a_s, a_r, x_s, x_r, f_s, f_r,
    s_s, s_r, y_s, y_r, z_s, z_r,
):
    i = lax.axis_index("ctx")
    j = lax.axis_index("kvh")
    z = lax.div(i, 4)
    r = lax.rem(i, 4)
    yh = lax.div(r, 2)
    c = lax.rem(i, 2)
    yl = lax.div(j, 4)
    x = lax.rem(j, 4)

    def ring(a):
        return lax.rem(a + 8, 8)

    sibling = {"ctx": i + 1 - 2 * c, "kvh": j}
    sides = [{"ctx": ring(z + 1) * 4 + r, "kvh": j}, {"ctx": ring(z - 1) * 4 + r, "kvh": j}]
    flip_i = i + 2 - 4 * yh
    flip_j = j + 4 - 8 * yl
    y_peers = [{"ctx": flip_i, "kvh": j}, {"ctx": i, "kvh": flip_j}, {"ctx": flip_i, "kvh": flip_j}]
    y_places = [(1 - yh, yl), (yh, 1 - yl), (1 - yh, 1 - yl)]
    x_places = [lax.rem(x + t, 4) for t in (1, 2, 3)]
    x_peers = [{"ctx": i, "kvh": yl * 4 + p} for p in x_places]

    barrier = pltpu.get_barrier_semaphore()
    for peer in [sibling] + y_peers + x_peers:
        pl.semaphore_signal(barrier, inc=1, device_id=peer, device_id_type=MESH)
    for t in range(1, 8):
        pl.semaphore_signal(
            barrier, inc=1, device_id={"ctx": ring(z + t) * 4 + r, "kvh": j}, device_id_type=MESH
        )

    kv[0, z, yh, c] = k_ref[...]
    kv[1, z, yh, c] = v_ref[...]
    for layer in range(2):
        w_all[layer, yl, z, c] = w_ref[layer, pl.ds(pl.multiple_of(yl * 80, 16), 80), :]
        for h in range(PAIRS):
            qs[layer * PAIRS + h] = q_ref[layer, :, h * 128 : (h + 1) * 128]
            dos[layer * PAIRS + h] = do_ref[layer, :, h * 128 : (h + 1) * 128]
    dkv[...] = jnp.zeros_like(dkv)
    pl.semaphore_wait(barrier, 14)

    def origin(way, n):
        step = n // 2 + 1
        return ring(z - step) if way == 0 else ring(z + step)

    reach = [2, 2, 1, 1, 3, 3, 4]

    def kv_arrival(way, n):
        return (way + n) % 2, ring(z - reach[n]) if way == 0 else ring(z + reach[n])

    def kv_hop(way, n):
        if n < 4:
            part, zz = (way + n) % 2, z
        else:
            part, zz = kv_arrival(way, n - 4 if n < 6 else 0)
        ref = kv.at[part, zz, yh, c]
        jump = 2 if n in (0, 1, 6) else 1
        target = {"ctx": (ring(z + jump) if way == 0 else ring(z - jump)) * 4 + r, "kvh": j}
        return send(ref, ref, kv_s.at[0], kv_r.at[way, n], target)

    def kv_wait(way, n):
        part, zz = kv_arrival(way, n)
        ref = kv.at[part, zz, yh, c]
        send(ref, ref, kv_s.at[0], kv_r.at[way, n], sides[way]).wait_recv()

    def kv_y(n, part, zz, place):
        ref = kv.at[part, zz, place, c]
        return send(ref, ref, ky_s.at[0], ky_r.at[n], y_peers[0])

    def kv_c(part, zz, place):
        ref = kv.at[part, zz, place, c]
        return send(ref, ref, kc_s.at[0], kc_r.at[0], sibling)

    def flip_key(zz, place, core):
        kt[zz, 2 * place + core] = kv[0, zz, place, core].astype(F32).T.astype(BF)

    def w_half(way, n):
        return lax.rem(yl + (1 if way == 1 and n == 6 else n % 2), 2)

    def w_send(layer, way, n):
        if n < 2:
            zz = z
        else:
            zz = ring(z - n // 2) if way == 0 else ring(z + n // 2)
        ref = w_all.at[layer, w_half(way, n), zz, c]
        return send(ref, ref, w_s.at[0], w_r.at[layer, way, n], sides[way])

    def w_sib(layer, half, zz):
        ref = w_all.at[layer, half, zz, c]
        return send(ref, ref, wc_s.at[0], wc_r.at[layer], sibling)

    def poll(layer, n):
        for way in range(2):
            zz = origin(way, n)
            half = w_half(way, n)
            ref = w_all.at[layer, half, zz, c]
            send(ref, ref, w_s.at[0], w_r.at[layer, way, n], sides[way]).wait_recv()
            if n <= 3 or (way == 0 and n == 4):
                w_send(layer, way, n + 2).start()
            if way == 1 and n == 5:
                w_send(layer, way, 6).start()
            w_sib(layer, half, zz).start()
        if layer == 0 and n in (5, 6):
            for way in range(2):
                w_send(1, way, n - 5).start()
            w_sib(1, w_half(0, n - 5), z).start()

    def w_swap(layer):
        return send(
            w_ref.at[layer, pl.ds(pl.multiple_of((1 - yl) * 80, 16), 80), :],
            w_all.at[layer, yl, z, c],
            ws_s.at[0],
            ws_r.at[layer],
            y_peers[1],
        )

    for n in range(4):
        for way in range(2):
            kv_hop(way, n).start()
    for n in range(2):
        kv_y(n, n, z, yh).start()
        kv_c(n, z, yh).start()
    w_swap(0).start()
    flip_key(z, yh, c)

    def pieces(n):
        if n < 0:
            return [(0, 0, z), (1, 1, z)]
        return [(2 + 2 * n + way,) + kv_arrival(way, n) for way in range(2)]

    def relay(n):
        for m, part, zz in pieces(n):
            kv_y(m, part, zz, 1 - yh).wait_recv()
            kv_c(part, zz, 1 - yh).start()
        for m, part, zz in pieces(n):
            if part == 0:
                if n >= 0:
                    flip_key(zz, yh, c)
                flip_key(zz, 1 - yh, c)

    def arrive(n):
        for way in range(2):
            kv_wait(way, n)
            if n == 0:
                kv_hop(way, 6).start()
            if n < 2:
                kv_hop(way, n + 4).start()
            part, zz = kv_arrival(way, n)
            kv_y(2 + 2 * n + way, part, zz, yh).start()
            kv_c(part, zz, yh).start()

    arrive(0)
    arrive(1)
    for way in range(2):
        w_send(0, way, 0).start()
    w_sib(0, w_half(0, 0), z).start()
    relay(-1)
    arrive(2)
    arrive(3)
    w_swap(0).wait_recv()
    for way in range(2):
        w_send(0, way, 1).start()
    w_sib(0, w_half(0, 1), z).start()
    relay(0)
    arrive(4)
    relay(1)
    arrive(5)
    arrive(6)
    relay(2)
    relay(3)
    poll(0, 0)
    relay(4)
    w_swap(1).start()
    relay(5)
    relay(6)
    poll(0, 1)
    others = kv.at[:, :, :, 1 - c]
    send(others, others, kc_s.at[0], kc_r.at[0], sibling).wait_recv()
    for zz in range(8):
        for spot in range(2):
            flip_key(zz, spot, 1 - c)
    poll(0, 2)
    w_swap(1).wait_recv()

    last = lax.div(z, 4)
    lane = lax.broadcasted_iota(jnp.int32, (SUB, 256), 1)
    place = z * 512 + r * 128 + lax.rem(lane, 128)

    def a_send(h, t):
        ref = a_all.at[pl.ds(2 * h, 2), yl, yh]
        return send(ref, ref, a_s.at[t], a_r.at[lax.div(h, 3), t], y_peers[t])

    def x_send(layer, t):
        return send(ct.at[layer, :, x_places[t]], xr.at[t, layer], x_s.at[0], x_r.at[layer], x_peers[t])

    def project(layer):
        part = pl.ds(0, 6) if layer == 0 else pl.ds(6, 4)
        for t, (ph, pw) in enumerate(y_places):
            ref = a_all.at[part, pw, ph]
            send(ref, ref, a_s.at[t], a_r.at[layer, t], y_peers[t]).wait_recv()
        ref = w_all.at[layer, :, :, 1 - c]
        send(ref, ref, wc_s.at[0], wc_r.at[layer], sibling).wait_recv()
        rows = [
            jnp.concatenate([a_all[layer * PAIRS + h, w].reshape(256, 128) for h in range(PAIRS)], axis=1)
            for w in range(2)
        ]
        for hi in range(2):
            total = dot_nt(w_all[layer, 0, 4 * hi : 4 * hi + 4].reshape(640, 640), rows[0])
            total = total + dot_nt(w_all[layer, 1, 4 * hi : 4 * hi + 4].reshape(640, 640), rows[1])
            ct[layer, hi] = total.astype(BF).reshape(4, 2, 80, 256)
        for t in range(3):
            x_send(layer, t).start()

    def pair(h, carry):
        two = pl.ds(2 * h, 2)
        query = qs[two].reshape(256, 128)
        cotangent = dos[two].reshape(256, 128)

        def forward(b, state, masked=False):
            m, total, weighted = state
            for n in range(PARTS):
                rows = pl.ds(n * SUB, SUB)
                zz = 4 * b + n // 4
                s = dot_nt(kv[0, zz, n // 2 % 2, n % 2], query)
                if masked:
                    key_place = lax.broadcasted_iota(jnp.int32, (SUB, 256), 0) + (b * BLOCK + n * SUB)
                    s = jnp.where(key_place <= place, s, LOWEST)
                d = dot_nt(kv[1, zz, n // 2 % 2, n % 2], cotangent)
                s = s.reshape(SUB // 8, 8, 256)
                peak = jnp.max(s, axis=0)
                e = jnp.exp2((s - peak[None]) * LOG2)
                part_total = jnp.sum(e, axis=0)
                part_weighted = jnp.sum(e * d.reshape(SUB // 8, 8, 256), axis=0)
                e_ref[b, rows] = e.reshape(SUB, 256)
                d_ref[b, rows] = d
                peaks[b, n] = peak
                new = jnp.maximum(m, peak)
                f0 = jnp.exp2((m - new) * LOG2)
                f1 = jnp.exp2((peak - new) * LOG2)
                total = total * f0 + part_total * f1
                weighted = weighted * f0 + part_weighted * f1
                m = new
            return m, total, weighted

        zero = jnp.zeros((8, 256), F32)
        state = lax.fori_loop(0, last, forward, (jnp.full((8, 256), LOWEST, F32), zero, zero))
        m8, total8, weighted8 = forward(last, state, True)
        for n, (layer, chunk) in enumerate(((0, 3), (0, 5), (1, 0), (1, 2), (1, 4))):
            pl.when(h == n)(lambda: poll(layer, chunk))
        m = jnp.max(m8, axis=0, keepdims=True)
        f = jnp.exp2((m8 - m) * LOG2)
        inverse = 1.0 / jnp.sum(total8 * f, axis=0, keepdims=True)
        delta = jnp.sum(weighted8 * f, axis=0, keepdims=True) * inverse

        def backward(b, dq):
            probs = []
            mixed = []
            for n in range(PARTS):
                rows = pl.ds(n * SUB, SUB)
                f = jnp.exp2((peaks[b, n] - m) * LOG2) * inverse
                p = (e_ref[b, rows].reshape(SUB // 8, 8, 256) * f[None]).reshape(SUB, 256)
                mixed.append((p * (d_ref[b, rows] - delta)).astype(BF))
                probs.append(p.astype(BF))
            probs = jnp.concatenate(probs, 0)
            mixed = jnp.concatenate(mixed, 0)
            here = pl.ds(4 * b, 4)
            shape = (4, 2, 2, 128, 128)
            dkv[1, here] += dot(probs, cotangent).reshape(shape)
            dkv[0, here] += dot(mixed, query).reshape(shape)
            keys = jnp.concatenate([kt[4 * b + n // 4, n % 4] for n in range(PARTS)], axis=1)
            return dq + dot(keys, mixed)

        dq = lax.fori_loop(0, last + 1, backward, jnp.zeros((128, 256), F32))
        for u in range(2):
            a_all[2 * h + u, yl, yh] = (dq[:, u * 128 : (u + 1) * 128].T * SCALE).astype(BF)
        for t in range(3):
            a_send(h, t).start()
        for n, (layer, chunk) in enumerate(((0, 4), (0, 6), (1, 1), (1, 3))):
            pl.when(h == n)(lambda: poll(layer, chunk))
        pl.when(h == 3)(lambda: project(0))
        return carry

    lax.fori_loop(0, PAIRS, pair, 0)

    def s_send(zz):
        return send(sb.at[:, zz], sbr.at[:, zz], s_s.at[zz], s_r.at[zz], sibling)

    def y_send(zz):
        return send(yb.at[:, zz], ybr.at[:, zz], y_s.at[zz], y_r.at[zz], y_peers[0])

    def stage_sibling(zz, carry):
        sb[0, zz] = (dkv[0, zz, :, 1 - c] * SCALE).astype(BF)
        sb[1, zz] = dkv[1, zz, :, 1 - c].astype(BF)
        s_send(zz).start()
        return carry

    lax.fori_loop(0, z + 1, stage_sibling, 0)

    def stage_y(zz, carry):
        s_send(zz).wait_recv()
        for n, scale in ((0, SCALE), (1, 1.0)):
            far = dkv[n, zz, 1 - yh, c] * scale + sbr[n, zz, 1 - yh].astype(F32)
            yb[n, zz] = far.astype(BF)
        y_send(zz).start()
        for n, scale in ((0, SCALE), (1, 1.0)):
            dkv[n, zz, yh, c] = dkv[n, zz, yh, c] * scale + sbr[n, zz, yh].astype(F32)
        return carry

    lax.fori_loop(0, z + 1, stage_y, 0)

    def finish(layer):
        ref = xr.at[:, layer]
        send(ref, ref, x_s.at[0], x_r.at[layer], sibling).wait_recv()
        total = ct[layer, :, x].astype(F32)
        for t in range(3):
            total = total + xr[t, layer].astype(F32)
        total = total.astype(BF)
        for half in range(2):
            fs[half, :, layer] = total[..., half * 128 : (half + 1) * 128]
        for t in range(3):
            f_send(layer, t).start()
        fr[layer, yh, :, yl] = fs[yh, yl, layer]

    def f_send(layer, t):
        ph, pw = y_places[t]
        return send(
            fs.at[ph, pw, layer], fr.at[layer, yh, :, yl], f_s.at[layer, t], f_r.at[layer, t], y_peers[t]
        )

    poll(1, 5)
    finish(0)
    poll(1, 6)
    project(1)

    def stage_z(zz, carry):
        y_send(zz).wait_recv()
        for n in range(2):
            near = dkv[n, zz, yh, c] + ybr[n, zz].astype(F32)
            dkv[n, zz, yh, c] = near
            zb[n, zz] = near.astype(BF)

        @pl.when(zz < z)
        def _():
            send(
                zb.at[:, zz], zr.at[:, z], z_s.at[zz], z_r.at[z], {"ctx": zz * 4 + r, "kvh": j}
            ).start()

        return carry

    early = jnp.minimum(z + 1, 5)
    lax.fori_loop(0, early, stage_z, 0)
    finish(1)
    lax.fori_loop(early, z + 1, stage_z, 0)

    def result(layer):
        for t in range(3):
            f_send(layer, t).wait_recv()
        out_ref[layer] = fr[layer].reshape(640, 128).astype(F32).T.astype(BF)

    result(0)

    def gather_z(zz, carry):
        send(zb.at[:, z], zr.at[:, zz], z_s.at[z], z_r.at[zz], sides[0]).wait_recv()
        for n in range(2):
            dkv[n, z, yh, c] += zr[n, zz].astype(F32)
        return carry

    lax.fori_loop(z + 1, 8, gather_z, 0)
    gk_ref[...] = dkv[0, z, yh, c].astype(BF)
    gv_ref[...] = dkv[1, z, yh, c].astype(BF)
    result(1)

    for sem, ref in (
        (kv_s.at[0], kv.at[0, pl.ds(0, 7), :, 0]),
        (ky_s.at[0], kv.at[0, :, :, 0]),
        (kc_s.at[0], kv.at[0]),
        (w_s.at[0], w_all.at[:, :, pl.ds(0, 7), 0]),
        (wc_s.at[0], w_all.at[:, :, :, 0]),
        (ws_s.at[0], w_all.at[:, 0, 0, 0]),
        (x_s.at[0], xr),
        (a_s.at[0], a_all.at[:, 0, 0]),
        (a_s.at[1], a_all.at[:, 0, 0]),
        (a_s.at[2], a_all.at[:, 0, 0]),
    ):
        send(ref, ref, sem, kc_r.at[0], sibling).wait_send()
    for layer in range(2):
        for t in range(3):
            f_send(layer, t).wait_send()

    def drain(zz, carry):
        s_send(zz).wait_send()
        y_send(zz).wait_send()

        @pl.when(zz < z)
        def _():
            send(zb.at[:, zz], zr.at[:, z], z_s.at[zz], z_r.at[z], sides[0]).wait_send()

        return carry

    lax.fori_loop(0, z + 1, drain, 0)


def body(queries, keys, values, grad_out, query_weight):
    dma = pltpu.SemaphoreType.DMA
    vmem = pltpu.VMEM
    return pl.pallas_call(
        kernel,
        out_shape=(
            jax.ShapeDtypeStruct((2, 128, 640), BF),
            jax.ShapeDtypeStruct((128, 128), BF),
            jax.ShapeDtypeStruct((128, 128), BF),
        ),
        in_specs=[pl.BlockSpec(memory_space=pltpu.VMEM)] * 5,
        out_specs=[pl.BlockSpec(memory_space=pltpu.VMEM)] * 3,
        scratch_shapes=[
            vmem((2, 8, 2, 2, 128, 128), BF),
            vmem((8, 4, 128, 128), BF),
            vmem((2, BLOCK, 256), F32),
            vmem((2, BLOCK, 256), F32),
            vmem((2, PARTS, 8, 256), F32),
            vmem((10, 128, 128), BF),
            vmem((10, 128, 128), BF),
            vmem((2, 8, 2, 2, 128, 128), F32),
            vmem((2, 2, 8, 2, 80, 640), BF),
            vmem((10, 2, 2, 128, 128), BF),
            vmem((2, 2, 4, 2, 80, 256), BF),
            vmem((3, 2, 2, 2, 80, 256), BF),
            vmem((2, 2, 2, 2, 80, 128), BF),
            vmem((2, 2, 2, 2, 80, 128), BF),
            vmem((2, 8, 2, 128, 128), BF),
            vmem((2, 8, 2, 128, 128), BF),
            vmem((2, 8, 128, 128), BF),
            vmem((2, 8, 128, 128), BF),
            vmem((2, 8, 128, 128), BF),
            vmem((2, 8, 128, 128), BF),
            dma((1,)), dma((2, 7)), dma((1,)), dma((16,)), dma((1,)), dma((1,)),
            dma((1,)), dma((2,)), dma((1,)), dma((2, 2, 7)), dma((1,)), dma((2,)),
            dma((3,)), dma((2, 3)), dma((1,)), dma((2,)), dma((2, 3)), dma((2, 3)),
            dma((8,)), dma((8,)), dma((8,)), dma((8,)), dma((8,)), dma((8,)),
        ],
        compiler_params=pltpu.CompilerParams(
            collective_id=0, has_side_effects=True, vmem_limit_bytes=56 << 20
        ),
    )(queries, keys, values, grad_out, query_weight)


def solution(mesh):
    cols = P(None, "ctx", "kvh")
    flat = P("ctx", "kvh")
    return jax.shard_map(
        body,
        mesh=mesh,
        in_specs=(cols, flat, flat, cols, cols),
        out_specs=(cols, flat, flat),
        check_vma=False,
    )
```

```python
import jax
import jax.numpy as jnp
from jax import lax
from jax.experimental import pallas as pl
from jax.experimental.pallas import tpu as pltpu
from jax.sharding import PartitionSpec as P

SCALE = 128 ** -0.5
LOG2 = SCALE * 1.4426950408889634
LOWEST = -1e30
NT = (((1,), (1,)), ((), ()))
MESH = pl.DeviceIdType.MESH
BF = jnp.bfloat16
F32 = jnp.float32
BLOCK = 2048
SUB = 128
PARTS = BLOCK // SUB
PAIRS = 5


def dot_nt(a, b):
    return lax.dot_general(a, b, NT, preferred_element_type=F32)


def dot(a, b):
    return jnp.dot(a, b, preferred_element_type=F32)


def send(src, dst, send_sem, recv_sem, device):
    return pltpu.make_async_remote_copy(
        src_ref=src,
        dst_ref=dst,
        send_sem=send_sem,
        recv_sem=recv_sem,
        device_id=device,
        device_id_type=MESH,
    )


def kernel(
    q_ref, k_ref, v_ref, do_ref, w_ref,
    turned_ref, both_ref,
    kv, kt, e_ref, d_ref, peaks, qs, dos, dkv, w_all, a_all, ct, xr, fs, fr,
    sb, sbr, yb, ybr, zb, zr,
    kv_s, kv_r, ky_s, ky_r, kc_s, kc_r,
    ws_s, ws_r, w_s, w_r, wc_s, wc_r,
    a_s, a_r, x_s, x_r, f_s, f_r,
    s_s, s_r, y_s, y_r, z_s, z_r,
):
    i = lax.axis_index("ctx")
    j = lax.axis_index("kvh")
    z = lax.div(i, 4)
    r = lax.rem(i, 4)
    yh = lax.div(r, 2)
    c = lax.rem(i, 2)
    yl = lax.div(j, 4)
    x = lax.rem(j, 4)

    def ring(a):
        return lax.rem(a + 8, 8)

    sibling = {"ctx": i + 1 - 2 * c, "kvh": j}
    sides = [{"ctx": ring(z + 1) * 4 + r, "kvh": j}, {"ctx": ring(z - 1) * 4 + r, "kvh": j}]
    flip_i = i + 2 - 4 * yh
    flip_j = j + 4 - 8 * yl
    y_peers = [{"ctx": flip_i, "kvh": j}, {"ctx": i, "kvh": flip_j}, {"ctx": flip_i, "kvh": flip_j}]
    y_places = [(1 - yh, yl), (yh, 1 - yl), (1 - yh, 1 - yl)]
    x_places = [lax.rem(x + t, 4) for t in (1, 2, 3)]
    x_peers = [{"ctx": i, "kvh": yl * 4 + p} for p in x_places]

    barrier = pltpu.get_barrier_semaphore()
    for peer in [sibling] + y_peers + x_peers:
        pl.semaphore_signal(barrier, inc=1, device_id=peer, device_id_type=MESH)
    for t in range(1, 8):
        pl.semaphore_signal(
            barrier, inc=1, device_id={"ctx": ring(z + t) * 4 + r, "kvh": j}, device_id_type=MESH
        )

    kv[0, z, yh, c] = k_ref[...]
    kv[1, z, yh, c] = v_ref[...]
    for layer in range(2):
        w_all[layer, yl, z, c] = w_ref[layer, pl.ds(pl.multiple_of(yl * 80, 16), 80), :]
        for h in range(PAIRS):
            qs[layer * PAIRS + h] = q_ref[layer, :, h * 128 : (h + 1) * 128]
            dos[layer * PAIRS + h] = do_ref[layer, :, h * 128 : (h + 1) * 128]
    dkv[...] = jnp.zeros_like(dkv)
    pl.semaphore_wait(barrier, 14)

    def shift(way, d):
        return ring(z - d) if way == 0 else ring(z + d)

    reach = [2, 2, 1, 1, 3, 3, 4]

    def kv_arrival(way, n):
        return (way + n) % 2, ring(z - reach[n]) if way == 0 else ring(z + reach[n])

    def kv_hop(way, n):
        if n < 4:
            part, zz = (way + n) % 2, z
        else:
            part, zz = kv_arrival(way, n - 4 if n < 6 else 0)
        ref = kv.at[part, zz, yh, c]
        jump = 2 if n in (0, 1, 6) else 1
        target = {"ctx": (ring(z + jump) if way == 0 else ring(z - jump)) * 4 + r, "kvh": j}
        return send(ref, ref, kv_s.at[0], kv_r.at[way, n], target)

    def kv_wait(way, n):
        part, zz = kv_arrival(way, n)
        ref = kv.at[part, zz, yh, c]
        send(ref, ref, kv_s.at[0], kv_r.at[way, n], sides[way]).wait_recv()

    def kv_y(n, part, zz, place):
        ref = kv.at[part, zz, place, c]
        return send(ref, ref, ky_s.at[0], ky_r.at[n], y_peers[0])

    def kv_c(part, zz, place):
        ref = kv.at[part, zz, place, c]
        return send(ref, ref, kc_s.at[0], kc_r.at[0], sibling)

    def flip_key(zz, place, core):
        kt[zz, 2 * place + core] = kv[0, zz, place, core].astype(F32).T.astype(BF)

    def w_half(layer, way, n):
        if layer == 0:
            return lax.rem(yl + (1 if way == 1 and n == 6 else n % 2), 2)
        return lax.rem(yl + way + n, 2)

    def w_ref_of(layer, way, n, zz):
        return w_all.at[layer, w_half(layer, way, n), zz, c]

    def w_send(layer, way, n):
        ref = w_ref_of(layer, way, n, z if n < 2 else shift(way, n // 2))
        return send(ref, ref, w_s.at[0], w_r.at[layer, way, n], sides[way])

    def w_sib(ref, group):
        return send(ref, ref, wc_s.at[0], wc_r.at[group], sibling)

    def own_weight(layer, n):
        for way in range(2):
            w_send(layer, way, n).start()
        w_sib(w_ref_of(layer, 0, n, z), layer).start()

    def poll(layer, n):
        for way in range(2):
            ref = w_ref_of(layer, way, n, shift(way, n // 2 + 1))
            send(ref, ref, w_s.at[0], w_r.at[layer, way, n], sides[way]).wait_recv()
            last_from = 5 if layer == 0 and way == 1 else 4
            if n < 4 or n == last_from:
                w_send(layer, way, 6 if n == last_from else n + 2).start()
            w_sib(ref, 2 if layer == 1 and n > 3 else layer).start()
        if layer == 0 and n in (3, 4):
            own_weight(1, n - 3)

    def w_swap(layer):
        return send(
            w_ref.at[layer, pl.ds(pl.multiple_of((1 - yl) * 80, 16), 80), :],
            w_all.at[layer, yl, z, c],
            ws_s.at[0],
            ws_r.at[layer],
            y_peers[1],
        )

    for n in range(4):
        for way in range(2):
            kv_hop(way, n).start()
    for n in range(2):
        kv_y(n, n, z, yh).start()
        kv_c(n, z, yh).start()
    w_swap(0).start()
    own_weight(0, 0)
    flip_key(z, yh, c)

    def pieces(n):
        if n < 0:
            return [(0, 0, z), (1, 1, z)]
        return [(2 + 2 * n + way,) + kv_arrival(way, n) for way in range(2)]

    def relay(n):
        for m, part, zz in pieces(n):
            kv_y(m, part, zz, 1 - yh).wait_recv()
            kv_c(part, zz, 1 - yh).start()
        for m, part, zz in pieces(n):
            if part == 0:
                if n >= 0:
                    flip_key(zz, yh, c)
                flip_key(zz, 1 - yh, c)

    def arrive(n):
        for way in range(2):
            kv_wait(way, n)
            if n == 0:
                kv_hop(way, 6).start()
            if n < 2:
                kv_hop(way, n + 4).start()
            part, zz = kv_arrival(way, n)
            kv_y(2 + 2 * n + way, part, zz, yh).start()
            kv_c(part, zz, yh).start()

    arrive(0)
    arrive(1)
    relay(-1)
    arrive(2)
    arrive(3)
    w_swap(0).wait_recv()
    own_weight(0, 1)
    relay(0)
    poll(0, 0)
    relay(1)
    arrive(4)
    arrive(5)
    arrive(6)
    relay(2)
    poll(0, 1)
    w_swap(1).start()
    relay(3)
    poll(0, 2)
    relay(4)
    w_swap(1).wait_recv()
    poll(0, 3)
    relay(5)
    relay(6)
    poll(0, 4)
    others = kv.at[:, :, :, 1 - c]
    send(others, others, kc_s.at[0], kc_r.at[0], sibling).wait_recv()
    for zz in range(8):
        for spot in range(2):
            flip_key(zz, spot, 1 - c)

    last = lax.div(z, 4)
    lane = lax.broadcasted_iota(jnp.int32, (SUB, 256), 1)
    place = z * 512 + r * 128 + lax.rem(lane, 128)

    def a_send(h, t):
        ref = a_all.at[pl.ds(2 * h, 2), yl, yh]
        return send(ref, ref, a_s.at[t], a_r.at[lax.div(h, 3), t], y_peers[t])

    def x_send(layer, t):
        return send(ct.at[layer, :, x_places[t]], xr.at[t, layer], x_s.at[0], x_r.at[layer], x_peers[t])

    def wait_rows(layer):
        part = pl.ds(0, 6) if layer == 0 else pl.ds(6, 4)
        for t, (ph, pw) in enumerate(y_places):
            ref = a_all.at[part, pw, ph]
            send(ref, ref, a_s.at[t], a_r.at[layer, t], y_peers[t]).wait_recv()

    def wait_weights(group, ref):
        send(ref, ref, wc_s.at[0], wc_r.at[group], sibling).wait_recv()

    def gathered(layer, w):
        return jnp.concatenate([a_all[layer * PAIRS + h, w].reshape(256, 128) for h in range(PAIRS)], axis=1)

    def first_layer():
        wait_rows(0)
        wait_weights(0, w_all.at[0, :, :, 1 - c])
        rows = [gathered(0, w) for w in range(2)]
        for hi in range(2):
            total = dot_nt(w_all[0, 0, 4 * hi : 4 * hi + 4].reshape(640, 640), rows[0])
            total = total + dot_nt(w_all[0, 1, 4 * hi : 4 * hi + 4].reshape(640, 640), rows[1])
            ct[0, hi] = total.astype(BF).reshape(4, 2, 80, 256)
        for t in range(3):
            x_send(0, t).start()

    def second_layer(planes):
        rows = [gathered(1, w) for w in range(2)]
        for zz in planes:
            total = dot_nt(w_all[1, 0, zz].reshape(160, 640), rows[0])
            total = total + dot_nt(w_all[1, 1, zz].reshape(160, 640), rows[1])
            hi = lax.div(zz, 4)
            p = lax.rem(zz, 4)
            ct[1, hi, p] = total.astype(BF).reshape(2, 80, 256)
            t = lax.rem(p - x + 4, 4)

            @pl.when(t > 0)
            def _():
                send(
                    ct.at[1, hi, p],
                    xr.at[t - 1, 1, hi],
                    x_s.at[0],
                    x_r.at[1],
                    {"ctx": i, "kvh": yl * 4 + p},
                ).start()

    def pair(h, carry):
        two = pl.ds(2 * h, 2)
        query = qs[two].reshape(256, 128)
        cotangent = dos[two].reshape(256, 128)

        def forward(b, state, masked=False):
            m, total, weighted = state
            for n in range(PARTS):
                rows = pl.ds(n * SUB, SUB)
                zz = 4 * b + n // 4
                s = dot_nt(kv[0, zz, n // 2 % 2, n % 2], query)
                if masked:
                    key_place = lax.broadcasted_iota(jnp.int32, (SUB, 256), 0) + (b * BLOCK + n * SUB)
                    s = jnp.where(key_place <= place, s, LOWEST)
                d = dot_nt(kv[1, zz, n // 2 % 2, n % 2], cotangent)
                s = s.reshape(SUB // 8, 8, 256)
                peak = jnp.max(s, axis=0)
                e = jnp.exp2((s - peak[None]) * LOG2)
                part_total = jnp.sum(e, axis=0)
                part_weighted = jnp.sum(e * d.reshape(SUB // 8, 8, 256), axis=0)
                e_ref[b, rows] = e.reshape(SUB, 256)
                d_ref[b, rows] = d
                peaks[b, n] = peak
                new = jnp.maximum(m, peak)
                f0 = jnp.exp2((m - new) * LOG2)
                f1 = jnp.exp2((peak - new) * LOG2)
                total = total * f0 + part_total * f1
                weighted = weighted * f0 + part_weighted * f1
                m = new
            return m, total, weighted

        zero = jnp.zeros((8, 256), F32)
        state = lax.fori_loop(0, last, forward, (jnp.full((8, 256), LOWEST, F32), zero, zero))
        m8, total8, weighted8 = forward(last, state, True)
        for n, (layer, chunk) in ((1, (0, 6)), (3, (1, 2)), (4, (1, 3))):
            pl.when(h == n)(lambda: poll(layer, chunk))
        m = jnp.max(m8, axis=0, keepdims=True)
        f = jnp.exp2((m8 - m) * LOG2)
        inverse = 1.0 / jnp.sum(total8 * f, axis=0, keepdims=True)
        delta = jnp.sum(weighted8 * f, axis=0, keepdims=True) * inverse

        def backward(b, dq):
            probs = []
            mixed = []
            for n in range(PARTS):
                rows = pl.ds(n * SUB, SUB)
                f = jnp.exp2((peaks[b, n] - m) * LOG2) * inverse
                p = (e_ref[b, rows].reshape(SUB // 8, 8, 256) * f[None]).reshape(SUB, 256)
                mixed.append((p * (d_ref[b, rows] - delta)).astype(BF))
                probs.append(p.astype(BF))
            probs = jnp.concatenate(probs, 0)
            mixed = jnp.concatenate(mixed, 0)
            here = pl.ds(4 * b, 4)
            shape = (4, 2, 2, 128, 128)
            dkv[1, here] += dot(probs, cotangent).reshape(shape)
            dkv[0, here] += dot(mixed, query).reshape(shape)
            keys = jnp.concatenate([kt[4 * b + n // 4, n % 4] for n in range(PARTS)], axis=1)
            return dq + dot(keys, mixed)

        dq = lax.fori_loop(0, last + 1, backward, jnp.zeros((128, 256), F32))
        for u in range(2):
            a_all[2 * h + u, yl, yh] = (dq[:, u * 128 : (u + 1) * 128].T * SCALE).astype(BF)
        for t in range(3):
            a_send(h, t).start()
        for n, (layer, chunk) in enumerate(((0, 5), (1, 0), (1, 1))):
            pl.when(h == n)(lambda: poll(layer, chunk))
        pl.when(h == 3)(first_layer)
        return carry

    lax.fori_loop(0, PAIRS, pair, 0)

    def s_send(zz):
        return send(sb.at[:, zz], sbr.at[:, zz], s_s.at[zz], s_r.at[zz], sibling)

    def y_send(zz):
        return send(yb.at[:, zz], ybr.at[:, zz], y_s.at[zz], y_r.at[zz], y_peers[0])

    def stage_sibling(zz, carry):
        sb[0, zz] = (dkv[0, zz, :, 1 - c] * SCALE).astype(BF)
        sb[1, zz] = dkv[1, zz, :, 1 - c].astype(BF)
        s_send(zz).start()
        return carry


    def stage_y(zz, carry):
        s_send(zz).wait_recv()
        for n, scale in ((0, SCALE), (1, 1.0)):
            far = dkv[n, zz, 1 - yh, c] * scale + sbr[n, zz, 1 - yh].astype(F32)
            yb[n, zz] = far.astype(BF)
        y_send(zz).start()
        for n, scale in ((0, SCALE), (1, 1.0)):
            dkv[n, zz, yh, c] = dkv[n, zz, yh, c] * scale + sbr[n, zz, yh].astype(F32)
        return carry

    def stage_z(zz, carry):
        y_send(zz).wait_recv()
        for n in range(2):
            near = dkv[n, zz, yh, c] + ybr[n, zz].astype(F32)
            dkv[n, zz, yh, c] = near
            zb[n, zz] = near.astype(BF)

        @pl.when(zz < z)
        def _():
            send(
                zb.at[:, zz], zr.at[:, z], z_s.at[zz], z_r.at[z], {"ctx": zz * 4 + r, "kvh": j}
            ).start()

        return carry

    def stage_both(zz, carry):
        stage_sibling(zz, carry)
        pl.when(zz > 1)(lambda: stage_y(zz - 2, None))
        return carry

    lax.fori_loop(0, z + 1, stage_both, 0)
    poll(1, 4)
    lax.fori_loop(jnp.maximum(z - 1, 0), z + 1, stage_y, 0)

    def finish(layer):
        ref = xr.at[:, layer]
        send(ref, ref, x_s.at[0], x_r.at[layer], sibling).wait_recv()
        total = ct[layer, :, x].astype(F32)
        for t in range(3):
            total = total + xr[t, layer].astype(F32)
        total = total.astype(BF)
        for half in range(2):
            fs[half, :, layer] = total[..., half * 128 : (half + 1) * 128]
        for t in range(3):
            f_send(layer, t).start()
        fr[layer, yh, :, yl] = fs[yh, yl, layer]

    def f_send(layer, t):
        ph, pw = y_places[t]
        return send(
            fs.at[ph, pw, layer], fr.at[layer, yh, :, yl], f_s.at[layer, t], f_r.at[layer, t], y_peers[t]
        )

    wait_rows(1)
    wait_weights(1, w_all.at[0, :, pl.ds(0, 5), 0])
    second_layer([z, shift(0, 1), shift(1, 1), shift(0, 2), shift(1, 2)])
    early = jnp.minimum(z + 1, 2)
    lax.fori_loop(0, early, stage_z, 0)
    poll(1, 5)
    poll(1, 6)
    wait_weights(2, w_all.at[0, :, pl.ds(0, 3), 0])
    second_layer([shift(0, 3), shift(1, 3), shift(0, 4)])
    finish(0)

    middle = jnp.minimum(z + 1, 6)
    lax.fori_loop(early, middle, stage_z, 0)
    finish(1)
    lax.fori_loop(middle, z + 1, stage_z, 0)

    def result(layer):
        for t in range(3):
            f_send(layer, t).wait_recv()
        turned_ref[layer] = fr[layer].reshape(640, 128)

    result(0)

    def gather_z(zz, carry):
        send(zb.at[:, z], zr.at[:, zz], z_s.at[z], z_r.at[zz], sides[0]).wait_recv()
        for n in range(2):
            dkv[n, z, yh, c] += zr[n, zz].astype(F32)
        return carry

    lax.fori_loop(z + 1, 8, gather_z, 0)
    for n in range(2):
        both_ref[n] = dkv[n, z, yh, c].astype(BF)
    result(1)

    for sem, ref in (
        (kv_s.at[0], kv.at[0, pl.ds(0, 7), :, 0]),
        (ky_s.at[0], kv.at[0, :, :, 0]),
        (kc_s.at[0], kv.at[0]),
        (w_s.at[0], w_all.at[:, :, pl.ds(0, 7), 0]),
        (wc_s.at[0], w_all.at[:, :, :, 0]),
        (ws_s.at[0], w_all.at[:, 0, 0, 0]),
        (x_s.at[0], xr),
        (a_s.at[0], a_all.at[:, 0, 0]),
        (a_s.at[1], a_all.at[:, 0, 0]),
        (a_s.at[2], a_all.at[:, 0, 0]),
    ):
        send(ref, ref, sem, kc_r.at[0], sibling).wait_send()
    for layer in range(2):
        for t in range(3):
            f_send(layer, t).wait_send()

    def drain(zz, carry):
        s_send(zz).wait_send()
        y_send(zz).wait_send()

        @pl.when(zz < z)
        def _():
            send(zb.at[:, zz], zr.at[:, z], z_s.at[zz], z_r.at[z], sides[0]).wait_send()

        return carry

    lax.fori_loop(0, z + 1, drain, 0)


def outputs_kernel(turned_ref, both_ref, out_ref, gk_ref, gv_ref):
    for layer in range(2):
        out_ref[layer] = turned_ref[layer].astype(F32).T.astype(BF)
    gk_ref[...] = both_ref[0]
    gv_ref[...] = both_ref[1]


def body(queries, keys, values, grad_out, query_weight):
    dma = pltpu.SemaphoreType.DMA
    vmem = pltpu.VMEM
    turned, both = pl.pallas_call(
        kernel,
        out_shape=(jax.ShapeDtypeStruct((2, 640, 128), BF), jax.ShapeDtypeStruct((2, 128, 128), BF)),
        in_specs=[pl.BlockSpec(memory_space=pltpu.VMEM)] * 5,
        out_specs=[pl.BlockSpec(memory_space=pltpu.VMEM)] * 2,
        scratch_shapes=[
            vmem((2, 8, 2, 2, 128, 128), BF),
            vmem((8, 4, 128, 128), BF),
            vmem((2, BLOCK, 256), F32),
            vmem((2, BLOCK, 256), F32),
            vmem((2, PARTS, 8, 256), F32),
            vmem((10, 128, 128), BF),
            vmem((10, 128, 128), BF),
            vmem((2, 8, 2, 2, 128, 128), F32),
            vmem((2, 2, 8, 2, 80, 640), BF),
            vmem((10, 2, 2, 128, 128), BF),
            vmem((2, 2, 4, 2, 80, 256), BF),
            vmem((3, 2, 2, 2, 80, 256), BF),
            vmem((2, 2, 2, 2, 80, 128), BF),
            vmem((2, 2, 2, 2, 80, 128), BF),
            vmem((2, 8, 2, 128, 128), BF),
            vmem((2, 8, 2, 128, 128), BF),
            vmem((2, 8, 128, 128), BF),
            vmem((2, 8, 128, 128), BF),
            vmem((2, 8, 128, 128), BF),
            vmem((2, 8, 128, 128), BF),
            dma((1,)), dma((2, 7)), dma((1,)), dma((16,)), dma((1,)), dma((1,)),
            dma((1,)), dma((2,)), dma((1,)), dma((2, 2, 7)), dma((1,)), dma((3,)),
            dma((3,)), dma((2, 3)), dma((1,)), dma((2,)), dma((2, 3)), dma((2, 3)),
            dma((8,)), dma((8,)), dma((8,)), dma((8,)), dma((8,)), dma((8,)),
        ],
        compiler_params=pltpu.CompilerParams(
            collective_id=0, has_side_effects=True, vmem_limit_bytes=56 << 20
        ),
    )(queries, keys, values, grad_out, query_weight)
    return pl.pallas_call(
        outputs_kernel,
        out_shape=(
            jax.ShapeDtypeStruct((2, 128, 640), BF),
            jax.ShapeDtypeStruct((128, 128), BF),
            jax.ShapeDtypeStruct((128, 128), BF),
        ),
        in_specs=[pl.BlockSpec(memory_space=pltpu.VMEM)] * 2,
        out_specs=[pl.BlockSpec(memory_space=pltpu.VMEM)] * 3,
    )(turned, both)


def solution(mesh):
    cols = P(None, "ctx", "kvh")
    flat = P("ctx", "kvh")
    return jax.shard_map(
        body,
        mesh=mesh,
        in_specs=(cols, flat, flat, cols, cols),
        out_specs=(cols, flat, flat),
        check_vma=False,
    )
```

```python
import jax
import jax.numpy as jnp
from jax import lax
from jax.experimental import pallas as pl
from jax.experimental.pallas import tpu as pltpu
from jax.sharding import PartitionSpec as P

SCALE = 128 ** -0.5
LOG2 = SCALE * 1.4426950408889634
LOWEST = -1e30
NT = (((1,), (1,)), ((), ()))
MESH = pl.DeviceIdType.MESH
BF = jnp.bfloat16
F32 = jnp.float32
BLOCK = 2048
SUB = 128
PARTS = BLOCK // SUB
PAIRS = 5


def dot_nt(a, b):
    return lax.dot_general(a, b, NT, preferred_element_type=F32)


def dot(a, b):
    return jnp.dot(a, b, preferred_element_type=F32)


def send(src, dst, send_sem, recv_sem, device):
    return pltpu.make_async_remote_copy(
        src_ref=src,
        dst_ref=dst,
        send_sem=send_sem,
        recv_sem=recv_sem,
        device_id=device,
        device_id_type=MESH,
    )


def kernel(
    q_ref, k_ref, v_ref, do_ref, w_ref,
    turned_ref, both_ref,
    kv, kt, e_ref, d_ref, peaks, qs, dos, dkv, w_all, a_all, ct, xr, fs, fr,
    sb, sbr, yb, ybr, zb, zr,
    kv_s, kv_r, ky_s, ky_r, kc_s, kc_r,
    ws_s, ws_r, w_s, w_r, wc_s, wc_r,
    a_s, a_r, x_s, x_r, f_s, f_r,
    s_s, s_r, y_s, y_r, z_s, z_r, in_s,
):
    i = lax.axis_index("ctx")
    j = lax.axis_index("kvh")
    z = lax.div(i, 4)
    r = lax.rem(i, 4)
    yh = lax.div(r, 2)
    c = lax.rem(i, 2)
    yl = lax.div(j, 4)
    x = lax.rem(j, 4)

    def ring(a):
        return lax.rem(a + 8, 8)

    sibling = {"ctx": i + 1 - 2 * c, "kvh": j}
    sides = [{"ctx": ring(z + 1) * 4 + r, "kvh": j}, {"ctx": ring(z - 1) * 4 + r, "kvh": j}]
    flip_i = i + 2 - 4 * yh
    flip_j = j + 4 - 8 * yl
    y_peers = [{"ctx": flip_i, "kvh": j}, {"ctx": i, "kvh": flip_j}, {"ctx": flip_i, "kvh": flip_j}]
    y_places = [(1 - yh, yl), (yh, 1 - yl), (1 - yh, 1 - yl)]
    x_places = [lax.rem(x + t, 4) for t in (1, 2, 3)]
    x_peers = [{"ctx": i, "kvh": yl * 4 + p} for p in x_places]

    barrier = pltpu.get_barrier_semaphore()
    for peer in [sibling] + y_peers + x_peers:
        pl.semaphore_signal(barrier, inc=1, device_id=peer, device_id_type=MESH)
    for t in range(1, 8):
        pl.semaphore_signal(
            barrier, inc=1, device_id={"ctx": ring(z + t) * 4 + r, "kvh": j}, device_id_type=MESH
        )

    loads = [
        pltpu.make_async_copy(k_ref, kv.at[0, z, yh, c], in_s.at[0]),
        pltpu.make_async_copy(v_ref, kv.at[1, z, yh, c], in_s.at[1]),
        pltpu.make_async_copy(
            w_ref.at[:, pl.ds(pl.multiple_of(yl * 80, 16), 80), :], w_all.at[:, yl, z, c], in_s.at[2]
        ),
    ]
    for load in loads:
        load.start()
    for layer in range(2):
        for h in range(PAIRS):
            column = pl.ds(h * 128, 128)
            g = layer * PAIRS + h
            pltpu.make_async_copy(q_ref.at[layer, :, column], qs.at[g], in_s.at[3]).start()
            pltpu.make_async_copy(do_ref.at[layer, :, column], dos.at[g], in_s.at[4]).start()
    dkv[...] = jnp.zeros_like(dkv)
    for load in loads:
        load.wait()
    pl.semaphore_wait(barrier, 14)

    def shift(way, d):
        return ring(z - d) if way == 0 else ring(z + d)

    reach = [2, 2, 1, 1, 3, 3, 4]

    def kv_arrival(way, n):
        return (way + n) % 2, ring(z - reach[n]) if way == 0 else ring(z + reach[n])

    def kv_hop(way, n):
        if n < 4:
            part, zz = (way + n) % 2, z
        else:
            part, zz = kv_arrival(way, n - 4 if n < 6 else 0)
        ref = kv.at[part, zz, yh, c]
        jump = 2 if n in (0, 1, 6) else 1
        target = {"ctx": (ring(z + jump) if way == 0 else ring(z - jump)) * 4 + r, "kvh": j}
        return send(ref, ref, kv_s.at[0], kv_r.at[way, n], target)

    def kv_wait(way, n):
        part, zz = kv_arrival(way, n)
        ref = kv.at[part, zz, yh, c]
        send(ref, ref, kv_s.at[0], kv_r.at[way, n], sides[way]).wait_recv()

    def kv_y(n, part, zz, place):
        ref = kv.at[part, zz, place, c]
        return send(ref, ref, ky_s.at[0], ky_r.at[n], y_peers[0])

    def kv_c(part, zz, place):
        ref = kv.at[part, zz, place, c]
        return send(ref, ref, kc_s.at[0], kc_r.at[0], sibling)

    def flip_key(zz, place, core):
        kt[zz, 2 * place + core] = kv[0, zz, place, core].astype(F32).T.astype(BF)

    def w_half(layer, way, n):
        if layer == 0:
            return lax.rem(yl + (1 if way == 1 and n == 6 else n % 2), 2)
        return lax.rem(yl + way + n, 2)

    def w_ref_of(layer, way, n, zz):
        return w_all.at[layer, w_half(layer, way, n), zz, c]

    def w_send(layer, way, n):
        ref = w_ref_of(layer, way, n, z if n < 2 else shift(way, n // 2))
        return send(ref, ref, w_s.at[0], w_r.at[layer, way, n], sides[way])

    def w_sib(ref, group):
        return send(ref, ref, wc_s.at[0], wc_r.at[group], sibling)

    def own_weight(layer, n):
        for way in range(2):
            w_send(layer, way, n).start()
        w_sib(w_ref_of(layer, 0, n, z), layer).start()

    def poll(layer, n):
        for way in range(2):
            ref = w_ref_of(layer, way, n, shift(way, n // 2 + 1))
            send(ref, ref, w_s.at[0], w_r.at[layer, way, n], sides[way]).wait_recv()
            last_from = 5 if layer == 0 and way == 1 else 4
            if n < 4 or n == last_from:
                w_send(layer, way, 6 if n == last_from else n + 2).start()
            w_sib(ref, 2 if layer == 1 and n > 3 else layer).start()
        if layer == 0 and n in (3, 4):
            own_weight(1, n - 3)

    def w_swap(layer):
        return send(
            w_ref.at[layer, pl.ds(pl.multiple_of((1 - yl) * 80, 16), 80), :],
            w_all.at[layer, yl, z, c],
            ws_s.at[0],
            ws_r.at[layer],
            y_peers[1],
        )

    for n in range(4):
        for way in range(2):
            kv_hop(way, n).start()
    for n in range(2):
        kv_y(n, n, z, yh).start()
        kv_c(n, z, yh).start()
    w_swap(0).start()
    own_weight(0, 0)
    flip_key(z, yh, c)

    def pieces(n):
        if n < 0:
            return [(0, 0, z), (1, 1, z)]
        return [(2 + 2 * n + way,) + kv_arrival(way, n) for way in range(2)]

    def relay(n):
        for m, part, zz in pieces(n):
            kv_y(m, part, zz, 1 - yh).wait_recv()
            kv_c(part, zz, 1 - yh).start()
        for m, part, zz in pieces(n):
            if part == 0:
                if n >= 0:
                    flip_key(zz, yh, c)
                flip_key(zz, 1 - yh, c)

    def arrive(n):
        for way in range(2):
            kv_wait(way, n)
            if n == 0:
                kv_hop(way, 6).start()
            if n < 2:
                kv_hop(way, n + 4).start()
            part, zz = kv_arrival(way, n)
            kv_y(2 + 2 * n + way, part, zz, yh).start()
            kv_c(part, zz, yh).start()

    arrive(0)
    arrive(1)
    relay(-1)
    arrive(2)
    arrive(3)
    w_swap(0).wait_recv()
    own_weight(0, 1)
    relay(0)
    poll(0, 0)
    relay(1)
    arrive(4)
    arrive(5)
    arrive(6)
    relay(2)
    poll(0, 1)
    w_swap(1).start()
    relay(3)
    poll(0, 2)
    relay(4)
    w_swap(1).wait_recv()
    poll(0, 3)
    relay(5)
    relay(6)
    poll(0, 4)
    others = kv.at[:, :, :, 1 - c]
    send(others, others, kc_s.at[0], kc_r.at[0], sibling).wait_recv()
    for zz in range(8):
        for spot in range(2):
            flip_key(zz, spot, 1 - c)

    pltpu.make_async_copy(qs, qs, in_s.at[3]).wait()
    pltpu.make_async_copy(dos, dos, in_s.at[4]).wait()
    last = lax.div(z, 4)
    lane = lax.broadcasted_iota(jnp.int32, (SUB, 256), 1)
    place = z * 512 + r * 128 + lax.rem(lane, 128)

    def a_send(h, t):
        ref = a_all.at[pl.ds(2 * h, 2), yl, yh]
        return send(ref, ref, a_s.at[t], a_r.at[lax.div(h, 3), t], y_peers[t])

    def x_send(layer, t):
        return send(ct.at[layer, :, x_places[t]], xr.at[t, layer], x_s.at[0], x_r.at[layer], x_peers[t])

    def wait_rows(layer):
        part = pl.ds(0, 6) if layer == 0 else pl.ds(6, 4)
        for t, (ph, pw) in enumerate(y_places):
            ref = a_all.at[part, pw, ph]
            send(ref, ref, a_s.at[t], a_r.at[layer, t], y_peers[t]).wait_recv()

    def wait_weights(group, ref):
        send(ref, ref, wc_s.at[0], wc_r.at[group], sibling).wait_recv()

    def gathered(layer, w):
        return jnp.concatenate([a_all[layer * PAIRS + h, w].reshape(256, 128) for h in range(PAIRS)], axis=1)

    def first_layer():
        wait_rows(0)
        wait_weights(0, w_all.at[0, :, :, 1 - c])
        rows = [gathered(0, w) for w in range(2)]
        for hi in range(2):
            total = dot_nt(w_all[0, 0, 4 * hi : 4 * hi + 4].reshape(640, 640), rows[0])
            total = total + dot_nt(w_all[0, 1, 4 * hi : 4 * hi + 4].reshape(640, 640), rows[1])
            ct[0, hi] = total.astype(BF).reshape(4, 2, 80, 256)
        for t in range(3):
            x_send(0, t).start()

    def second_layer(planes):
        rows = [gathered(1, w) for w in range(2)]
        for zz in planes:
            total = dot_nt(w_all[1, 0, zz].reshape(160, 640), rows[0])
            total = total + dot_nt(w_all[1, 1, zz].reshape(160, 640), rows[1])
            hi = lax.div(zz, 4)
            p = lax.rem(zz, 4)
            ct[1, hi, p] = total.astype(BF).reshape(2, 80, 256)
            t = lax.rem(p - x + 4, 4)

            @pl.when(t > 0)
            def _():
                send(
                    ct.at[1, hi, p],
                    xr.at[t - 1, 1, hi],
                    x_s.at[0],
                    x_r.at[1],
                    {"ctx": i, "kvh": yl * 4 + p},
                ).start()

    def pair(h, carry):
        two = pl.ds(2 * h, 2)
        query = qs[two].reshape(256, 128)
        cotangent = dos[two].reshape(256, 128)

        def forward(b, state, masked=False):
            m, total, weighted = state
            for n in range(PARTS):
                rows = pl.ds(n * SUB, SUB)
                zz = 4 * b + n // 4
                s = dot_nt(kv[0, zz, n // 2 % 2, n % 2], query)
                if masked:
                    key_place = lax.broadcasted_iota(jnp.int32, (SUB, 256), 0) + (b * BLOCK + n * SUB)
                    s = jnp.where(key_place <= place, s, LOWEST)
                d = dot_nt(kv[1, zz, n // 2 % 2, n % 2], cotangent)
                s = s.reshape(SUB // 8, 8, 256)
                peak = jnp.max(s, axis=0)
                e = jnp.exp2((s - peak[None]) * LOG2)
                part_total = jnp.sum(e, axis=0)
                part_weighted = jnp.sum(e * d.reshape(SUB // 8, 8, 256), axis=0)
                e_ref[b, rows] = e.reshape(SUB, 256)
                d_ref[b, rows] = d
                peaks[b, n] = peak
                new = jnp.maximum(m, peak)
                f0 = jnp.exp2((m - new) * LOG2)
                f1 = jnp.exp2((peak - new) * LOG2)
                total = total * f0 + part_total * f1
                weighted = weighted * f0 + part_weighted * f1
                m = new
            return m, total, weighted

        zero = jnp.zeros((8, 256), F32)
        state = lax.fori_loop(0, last, forward, (jnp.full((8, 256), LOWEST, F32), zero, zero))
        m8, total8, weighted8 = forward(last, state, True)
        for n, (layer, chunk) in enumerate(((0, 5), (0, 6), (1, 0), (1, 1), (1, 3))):
            pl.when(h == n)(lambda: poll(layer, chunk))
        m = jnp.max(m8, axis=0, keepdims=True)
        f = jnp.exp2((m8 - m) * LOG2)
        inverse = 1.0 / jnp.sum(total8 * f, axis=0, keepdims=True)
        delta = jnp.sum(weighted8 * f, axis=0, keepdims=True) * inverse

        def backward(b, dq):
            probs = []
            mixed = []
            for n in range(PARTS):
                rows = pl.ds(n * SUB, SUB)
                f = jnp.exp2((peaks[b, n] - m) * LOG2) * inverse
                p = (e_ref[b, rows].reshape(SUB // 8, 8, 256) * f[None]).reshape(SUB, 256)
                mixed.append((p * (d_ref[b, rows] - delta)).astype(BF))
                probs.append(p.astype(BF))
            probs = jnp.concatenate(probs, 0)
            mixed = jnp.concatenate(mixed, 0)
            here = pl.ds(4 * b, 4)
            shape = (4, 2, 2, 128, 128)
            dkv[1, here] += dot(probs, cotangent).reshape(shape)
            dkv[0, here] += dot(mixed, query).reshape(shape)
            keys = jnp.concatenate([kt[4 * b + n // 4, n % 4] for n in range(PARTS)], axis=1)
            return dq + dot(keys, mixed)

        dq = lax.fori_loop(0, last + 1, backward, jnp.zeros((128, 256), F32))
        for u in range(2):
            a_all[2 * h + u, yl, yh] = (dq[:, u * 128 : (u + 1) * 128].T * SCALE).astype(BF)
        for t in range(3):
            a_send(h, t).start()
        for n, (layer, chunk) in ((3, (1, 2)),):
            pl.when(h == n)(lambda: poll(layer, chunk))
        pl.when(h == 3)(first_layer)
        return carry

    lax.fori_loop(0, PAIRS, pair, 0)

    def s_send(zz):
        return send(sb.at[:, zz], sbr.at[:, zz], s_s.at[zz], s_r.at[zz], sibling)

    def y_send(zz):
        return send(yb.at[:, zz], ybr.at[:, zz], y_s.at[zz], y_r.at[zz], y_peers[0])

    def stage_sibling(zz, carry):
        sb[0, zz] = (dkv[0, zz, :, 1 - c] * SCALE).astype(BF)
        sb[1, zz] = dkv[1, zz, :, 1 - c].astype(BF)
        s_send(zz).start()
        return carry


    def stage_y(zz, carry):
        s_send(zz).wait_recv()
        for n, scale in ((0, SCALE), (1, 1.0)):
            far = dkv[n, zz, 1 - yh, c] * scale + sbr[n, zz, 1 - yh].astype(F32)
            yb[n, zz] = far.astype(BF)
        y_send(zz).start()
        for n, scale in ((0, SCALE), (1, 1.0)):
            dkv[n, zz, yh, c] = dkv[n, zz, yh, c] * scale + sbr[n, zz, yh].astype(F32)
        return carry

    def stage_z(zz, carry):
        y_send(zz).wait_recv()
        for n in range(2):
            near = dkv[n, zz, yh, c] + ybr[n, zz].astype(F32)
            dkv[n, zz, yh, c] = near
            zb[n, zz] = near.astype(BF)

        @pl.when(zz < z)
        def _():
            send(
                zb.at[:, zz], zr.at[:, z], z_s.at[zz], z_r.at[z], {"ctx": zz * 4 + r, "kvh": j}
            ).start()

        return carry

    def stage_both(zz, carry):
        stage_sibling(zz, carry)
        pl.when(zz > 1)(lambda: stage_y(zz - 2, None))
        return carry

    lax.fori_loop(0, z + 1, stage_both, 0)
    poll(1, 4)
    lax.fori_loop(jnp.maximum(z - 1, 0), z + 1, stage_y, 0)

    def finish(layer):
        ref = xr.at[:, layer]
        send(ref, ref, x_s.at[0], x_r.at[layer], sibling).wait_recv()
        total = ct[layer, :, x].astype(F32)
        for t in range(3):
            total = total + xr[t, layer].astype(F32)
        total = total.astype(BF)
        for half in range(2):
            fs[half, :, layer] = total[..., half * 128 : (half + 1) * 128]
        for t in range(3):
            f_send(layer, t).start()
        fr[layer, yh, :, yl] = fs[yh, yl, layer]

    def f_send(layer, t):
        ph, pw = y_places[t]
        return send(
            fs.at[ph, pw, layer], fr.at[layer, yh, :, yl], f_s.at[layer, t], f_r.at[layer, t], y_peers[t]
        )

    wait_rows(1)
    wait_weights(1, w_all.at[0, :, pl.ds(0, 5), 0])
    second_layer([z, shift(0, 1), shift(1, 1), shift(0, 2), shift(1, 2)])
    early = jnp.minimum(z + 1, 2)
    lax.fori_loop(0, early, stage_z, 0)
    poll(1, 5)
    poll(1, 6)
    wait_weights(2, w_all.at[0, :, pl.ds(0, 3), 0])
    second_layer([shift(0, 3), shift(1, 3), shift(0, 4)])
    finish(0)

    middle = jnp.minimum(z + 1, 6)
    lax.fori_loop(early, middle, stage_z, 0)
    finish(1)
    lax.fori_loop(middle, z + 1, stage_z, 0)

    def result(layer):
        for t in range(3):
            f_send(layer, t).wait_recv()
        turned_ref[layer] = fr[layer].reshape(640, 128)

    result(0)

    def gather_z(zz, carry):
        send(zb.at[:, z], zr.at[:, zz], z_s.at[z], z_r.at[zz], sides[0]).wait_recv()
        for n in range(2):
            dkv[n, z, yh, c] += zr[n, zz].astype(F32)
        return carry

    lax.fori_loop(z + 1, 8, gather_z, 0)
    for n in range(2):
        both_ref[n] = dkv[n, z, yh, c].astype(BF)
    result(1)

    for sem, ref in (
        (kv_s.at[0], kv.at[0, pl.ds(0, 7), :, 0]),
        (ky_s.at[0], kv.at[0, :, :, 0]),
        (kc_s.at[0], kv.at[0]),
        (w_s.at[0], w_all.at[:, :, pl.ds(0, 7), 0]),
        (wc_s.at[0], w_all.at[:, :, :, 0]),
        (ws_s.at[0], w_all.at[:, 0, 0, 0]),
        (x_s.at[0], xr),
        (a_s.at[0], a_all.at[:, 0, 0]),
        (a_s.at[1], a_all.at[:, 0, 0]),
        (a_s.at[2], a_all.at[:, 0, 0]),
    ):
        send(ref, ref, sem, kc_r.at[0], sibling).wait_send()
    for layer in range(2):
        for t in range(3):
            f_send(layer, t).wait_send()

    def drain(zz, carry):
        s_send(zz).wait_send()
        y_send(zz).wait_send()

        @pl.when(zz < z)
        def _():
            send(zb.at[:, zz], zr.at[:, z], z_s.at[zz], z_r.at[z], sides[0]).wait_send()

        return carry

    lax.fori_loop(0, z + 1, drain, 0)


def outputs_kernel(turned_ref, both_ref, out_ref, gk_ref, gv_ref):
    for layer in range(2):
        out_ref[layer] = turned_ref[layer].astype(F32).T.astype(BF)
    gk_ref[...] = both_ref[0]
    gv_ref[...] = both_ref[1]


def body(queries, keys, values, grad_out, query_weight):
    dma = pltpu.SemaphoreType.DMA
    vmem = pltpu.VMEM
    turned, both = pl.pallas_call(
        kernel,
        out_shape=(jax.ShapeDtypeStruct((2, 640, 128), BF), jax.ShapeDtypeStruct((2, 128, 128), BF)),
        in_specs=[pl.BlockSpec(memory_space=pl.ANY)] * 5,
        out_specs=[pl.BlockSpec(memory_space=pltpu.VMEM)] * 2,
        scratch_shapes=[
            vmem((2, 8, 2, 2, 128, 128), BF),
            vmem((8, 4, 128, 128), BF),
            vmem((2, BLOCK, 256), F32),
            vmem((2, BLOCK, 256), F32),
            vmem((2, PARTS, 8, 256), F32),
            vmem((10, 128, 128), BF),
            vmem((10, 128, 128), BF),
            vmem((2, 8, 2, 2, 128, 128), F32),
            vmem((2, 2, 8, 2, 80, 640), BF),
            vmem((10, 2, 2, 128, 128), BF),
            vmem((2, 2, 4, 2, 80, 256), BF),
            vmem((3, 2, 2, 2, 80, 256), BF),
            vmem((2, 2, 2, 2, 80, 128), BF),
            vmem((2, 2, 2, 2, 80, 128), BF),
            vmem((2, 8, 2, 128, 128), BF),
            vmem((2, 8, 2, 128, 128), BF),
            vmem((2, 8, 128, 128), BF),
            vmem((2, 8, 128, 128), BF),
            vmem((2, 8, 128, 128), BF),
            vmem((2, 8, 128, 128), BF),
            dma((1,)), dma((2, 7)), dma((1,)), dma((16,)), dma((1,)), dma((1,)),
            dma((1,)), dma((2,)), dma((1,)), dma((2, 2, 7)), dma((1,)), dma((3,)),
            dma((3,)), dma((2, 3)), dma((1,)), dma((2,)), dma((2, 3)), dma((2, 3)),
            dma((8,)), dma((8,)), dma((8,)), dma((8,)), dma((8,)), dma((8,)), dma((5,)),
        ],
        compiler_params=pltpu.CompilerParams(
            collective_id=0, has_side_effects=True, vmem_limit_bytes=56 << 20
        ),
    )(queries, keys, values, grad_out, query_weight)
    return pl.pallas_call(
        outputs_kernel,
        out_shape=(
            jax.ShapeDtypeStruct((2, 128, 640), BF),
            jax.ShapeDtypeStruct((128, 128), BF),
            jax.ShapeDtypeStruct((128, 128), BF),
        ),
        in_specs=[pl.BlockSpec(memory_space=pltpu.VMEM)] * 2,
        out_specs=[pl.BlockSpec(memory_space=pltpu.VMEM)] * 3,
    )(turned, both)


def solution(mesh):
    cols = P(None, "ctx", "kvh")
    flat = P("ctx", "kvh")
    return jax.shard_map(
        body,
        mesh=mesh,
        in_specs=(cols, flat, flat, cols, cols),
        out_specs=(cols, flat, flat),
        check_vma=False,
    )
```

```python
import jax
import jax.numpy as jnp
from jax import lax
from jax.experimental import pallas as pl
from jax.experimental.pallas import tpu as pltpu
from jax.sharding import PartitionSpec as P

SCALE = 128 ** -0.5
LOG2 = SCALE * 1.4426950408889634
LOWEST = -1e30
NT = (((1,), (1,)), ((), ()))
MESH = pl.DeviceIdType.MESH
BF = jnp.bfloat16
F32 = jnp.float32
BLOCK = 2048
SUB = 128
PARTS = BLOCK // SUB
PAIRS = 5


def dot_nt(a, b):
    return lax.dot_general(a, b, NT, preferred_element_type=F32)


def dot(a, b):
    return jnp.dot(a, b, preferred_element_type=F32)


def send(src, dst, send_sem, recv_sem, device):
    return pltpu.make_async_remote_copy(
        src_ref=src,
        dst_ref=dst,
        send_sem=send_sem,
        recv_sem=recv_sem,
        device_id=device,
        device_id_type=MESH,
    )


def kernel(
    q_ref, k_ref, v_ref, do_ref, w_ref,
    turned_ref, both_ref,
    kv, kt, e_ref, d_ref, peaks, qs, dos, dkv, w_all, a_all, ct, xr, fs, fr,
    sb, sbr, yb, ybr, zb, zr,
    kv_s, kv_r, ky_s, ky_r, kc_s, kc_r,
    ws_s, ws_r, w_s, w_r, wc_s, wc_r,
    a_s, a_r, x_s, x_r, f_s, f_r,
    s_s, s_r, y_s, y_r, z_s, z_r, in_s,
):
    i = lax.axis_index("ctx")
    j = lax.axis_index("kvh")
    z = lax.div(i, 4)
    r = lax.rem(i, 4)
    yh = lax.div(r, 2)
    c = lax.rem(i, 2)
    yl = lax.div(j, 4)
    x = lax.rem(j, 4)

    def ring(a):
        return lax.rem(a + 8, 8)

    sibling = {"ctx": i + 1 - 2 * c, "kvh": j}
    sides = [{"ctx": ring(z + 1) * 4 + r, "kvh": j}, {"ctx": ring(z - 1) * 4 + r, "kvh": j}]
    flip_i = i + 2 - 4 * yh
    flip_j = j + 4 - 8 * yl
    y_peers = [{"ctx": flip_i, "kvh": j}, {"ctx": i, "kvh": flip_j}, {"ctx": flip_i, "kvh": flip_j}]
    y_places = [(1 - yh, yl), (yh, 1 - yl), (1 - yh, 1 - yl)]
    x_places = [lax.rem(x + t, 4) for t in (1, 2, 3)]
    x_peers = [{"ctx": i, "kvh": yl * 4 + p} for p in x_places]

    barrier = pltpu.get_barrier_semaphore()
    for peer in [sibling] + y_peers + x_peers:
        pl.semaphore_signal(barrier, inc=1, device_id=peer, device_id_type=MESH)
    for t in range(1, 8):
        pl.semaphore_signal(
            barrier, inc=1, device_id={"ctx": ring(z + t) * 4 + r, "kvh": j}, device_id_type=MESH
        )

    loads = [
        pltpu.make_async_copy(k_ref, kv.at[0, z, yh, c], in_s.at[0]),
        pltpu.make_async_copy(v_ref, kv.at[1, z, yh, c], in_s.at[1]),
        pltpu.make_async_copy(
            w_ref.at[:, pl.ds(pl.multiple_of(yl * 80, 16), 80), :], w_all.at[:, yl, z, c], in_s.at[2]
        ),
    ]
    for load in loads:
        load.start()
    for layer in range(2):
        for h in range(PAIRS):
            column = pl.ds(h * 128, 128)
            g = layer * PAIRS + h
            pltpu.make_async_copy(q_ref.at[layer, :, column], qs.at[g], in_s.at[3]).start()
            pltpu.make_async_copy(do_ref.at[layer, :, column], dos.at[g], in_s.at[4]).start()
    dkv[...] = jnp.zeros_like(dkv)
    for load in loads:
        load.wait()
    pl.semaphore_wait(barrier, 14)

    def shift(way, d):
        return ring(z - d) if way == 0 else ring(z + d)

    reach = [2, 2, 1, 1, 3, 3, 4]

    def kv_arrival(way, n):
        return (way + n) % 2, ring(z - reach[n]) if way == 0 else ring(z + reach[n])

    def kv_hop(way, n):
        if n < 4:
            part, zz = (way + n) % 2, z
        else:
            part, zz = kv_arrival(way, n - 4 if n < 6 else 0)
        ref = kv.at[part, zz, yh, c]
        jump = 2 if n in (0, 1, 6) else 1
        target = {"ctx": (ring(z + jump) if way == 0 else ring(z - jump)) * 4 + r, "kvh": j}
        return send(ref, ref, kv_s.at[0], kv_r.at[way, n], target)

    def kv_wait(way, n):
        part, zz = kv_arrival(way, n)
        ref = kv.at[part, zz, yh, c]
        send(ref, ref, kv_s.at[0], kv_r.at[way, n], sides[way]).wait_recv()

    def kv_y(n, part, zz, place):
        ref = kv.at[part, zz, place, c]
        return send(ref, ref, ky_s.at[0], ky_r.at[n], y_peers[0])

    def kv_c(part, zz, place):
        ref = kv.at[part, zz, place, c]
        return send(ref, ref, kc_s.at[0], kc_r.at[0], sibling)

    def flip_key(zz, place, core):
        kt[zz, 2 * place + core] = kv[0, zz, place, core].astype(F32).T.astype(BF)

    def w_half(layer, way, n):
        if layer == 0:
            return lax.rem(yl + (1 if way == 1 and n == 6 else n % 2), 2)
        return lax.rem(yl + way + n, 2)

    def w_ref_of(layer, way, n, zz):
        return w_all.at[layer, w_half(layer, way, n), zz, c]

    def w_send(layer, way, n):
        ref = w_ref_of(layer, way, n, z if n < 2 else shift(way, n // 2))
        return send(ref, ref, w_s.at[0], w_r.at[layer, way, n], sides[way])

    def w_sib(ref, group):
        return send(ref, ref, wc_s.at[0], wc_r.at[group], sibling)

    def own_weight(layer, n):
        for way in range(2):
            w_send(layer, way, n).start()
        w_sib(w_ref_of(layer, 0, n, z), layer).start()

    def poll(layer, n):
        for way in range(2):
            ref = w_ref_of(layer, way, n, shift(way, n // 2 + 1))
            send(ref, ref, w_s.at[0], w_r.at[layer, way, n], sides[way]).wait_recv()
            last_from = 5 if layer == 0 and way == 1 else 4
            if n < 4 or n == last_from:
                w_send(layer, way, 6 if n == last_from else n + 2).start()
            w_sib(ref, 2 if layer == 1 and n > 3 else layer).start()
        if layer == 0 and n in (3, 4):
            own_weight(1, n - 3)

    def w_swap(layer):
        return send(
            w_ref.at[layer, pl.ds(pl.multiple_of((1 - yl) * 80, 16), 80), :],
            w_all.at[layer, yl, z, c],
            ws_s.at[0],
            ws_r.at[layer],
            y_peers[1],
        )

    for n in range(4):
        for way in range(2):
            kv_hop(way, n).start()
    for n in range(2):
        kv_y(n, n, z, yh).start()
        kv_c(n, z, yh).start()
    w_swap(0).start()
    own_weight(0, 0)
    flip_key(z, yh, c)

    def pieces(n):
        if n < 0:
            return [(0, 0, z), (1, 1, z)]
        return [(2 + 2 * n + way,) + kv_arrival(way, n) for way in range(2)]

    def relay(n):
        for m, part, zz in pieces(n):
            kv_y(m, part, zz, 1 - yh).wait_recv()
            kv_c(part, zz, 1 - yh).start()
        for m, part, zz in pieces(n):
            if part == 0:
                if n >= 0:
                    flip_key(zz, yh, c)
                flip_key(zz, 1 - yh, c)

    def arrive(n):
        for way in range(2):
            kv_wait(way, n)
            if n == 0:
                kv_hop(way, 6).start()
            if n < 2:
                kv_hop(way, n + 4).start()
            part, zz = kv_arrival(way, n)
            kv_y(2 + 2 * n + way, part, zz, yh).start()
            kv_c(part, zz, yh).start()

    arrive(0)
    arrive(1)
    relay(-1)
    arrive(2)
    arrive(3)
    w_swap(0).wait_recv()
    own_weight(0, 1)
    relay(0)
    poll(0, 0)
    relay(1)
    arrive(4)
    arrive(5)
    arrive(6)
    relay(2)
    poll(0, 1)
    w_swap(1).start()
    relay(3)
    poll(0, 2)
    relay(4)
    w_swap(1).wait_recv()
    poll(0, 3)
    relay(5)
    relay(6)
    poll(0, 4)
    others = kv.at[:, :, :, 1 - c]
    send(others, others, kc_s.at[0], kc_r.at[0], sibling).wait_recv()
    for zz in range(8):
        for spot in range(2):
            flip_key(zz, spot, 1 - c)

    pltpu.make_async_copy(qs, qs, in_s.at[3]).wait()
    pltpu.make_async_copy(dos, dos, in_s.at[4]).wait()
    last = lax.div(z, 4)
    lane = lax.broadcasted_iota(jnp.int32, (SUB, 256), 1)
    place = z * 512 + r * 128 + lax.rem(lane, 128)

    def a_send(h, t):
        ref = a_all.at[pl.ds(2 * h, 2), yl, yh]
        return send(ref, ref, a_s.at[t], a_r.at[lax.div(h, 3), t], y_peers[t])

    def x_send(layer, t):
        return send(ct.at[layer, :, x_places[t]], xr.at[t, layer], x_s.at[0], x_r.at[layer], x_peers[t])

    def wait_rows(layer):
        part = pl.ds(0, 6) if layer == 0 else pl.ds(6, 4)
        for t, (ph, pw) in enumerate(y_places):
            ref = a_all.at[part, pw, ph]
            send(ref, ref, a_s.at[t], a_r.at[layer, t], y_peers[t]).wait_recv()

    def wait_weights(group, ref):
        send(ref, ref, wc_s.at[0], wc_r.at[group], sibling).wait_recv()

    def gathered(layer, w):
        return jnp.concatenate([a_all[layer * PAIRS + h, w].reshape(256, 128) for h in range(PAIRS)], axis=1)

    def first_layer():
        wait_rows(0)
        wait_weights(0, w_all.at[0, :, :, 1 - c])
        rows = [gathered(0, w) for w in range(2)]
        for hi in range(2):
            total = dot_nt(w_all[0, 0, 4 * hi : 4 * hi + 4].reshape(640, 640), rows[0])
            total = total + dot_nt(w_all[0, 1, 4 * hi : 4 * hi + 4].reshape(640, 640), rows[1])
            ct[0, hi] = total.astype(BF).reshape(4, 2, 80, 256)
        for t in range(3):
            x_send(0, t).start()

    def second_layer(planes):
        rows = [gathered(1, w) for w in range(2)]
        for zz in planes:
            total = dot_nt(w_all[1, 0, zz].reshape(160, 640), rows[0])
            total = total + dot_nt(w_all[1, 1, zz].reshape(160, 640), rows[1])
            hi = lax.div(zz, 4)
            p = lax.rem(zz, 4)
            ct[1, hi, p] = total.astype(BF).reshape(2, 80, 256)
            t = lax.rem(p - x + 4, 4)

            @pl.when(t > 0)
            def _():
                send(
                    ct.at[1, hi, p],
                    xr.at[t - 1, 1, hi],
                    x_s.at[0],
                    x_r.at[1],
                    {"ctx": i, "kvh": yl * 4 + p},
                ).start()

    def pair(h, carry):
        two = pl.ds(2 * h, 2)
        query = qs[two].reshape(256, 128)
        cotangent = dos[two].reshape(256, 128)

        def forward(b, state, masked=False):
            m, total, weighted = state
            for n in range(PARTS):
                rows = pl.ds(n * SUB, SUB)
                zz = 4 * b + n // 4
                s = dot_nt(kv[0, zz, n // 2 % 2, n % 2], query)
                if masked:
                    key_place = lax.broadcasted_iota(jnp.int32, (SUB, 256), 0) + (b * BLOCK + n * SUB)
                    s = jnp.where(key_place <= place, s, LOWEST)
                d = dot_nt(kv[1, zz, n // 2 % 2, n % 2], cotangent)
                s = s.reshape(SUB // 8, 8, 256)
                peak = jnp.max(s, axis=0)
                e = jnp.exp2((s - peak[None]) * LOG2)
                part_total = jnp.sum(e, axis=0)
                part_weighted = jnp.sum(e * d.reshape(SUB // 8, 8, 256), axis=0)
                e_ref[b, rows] = e.reshape(SUB, 256)
                d_ref[b, rows] = d
                peaks[b, n] = peak
                new = jnp.maximum(m, peak)
                f0 = jnp.exp2((m - new) * LOG2)
                f1 = jnp.exp2((peak - new) * LOG2)
                total = total * f0 + part_total * f1
                weighted = weighted * f0 + part_weighted * f1
                m = new
            return m, total, weighted

        zero = jnp.zeros((8, 256), F32)
        state = lax.fori_loop(0, last, forward, (jnp.full((8, 256), LOWEST, F32), zero, zero))
        m8, total8, weighted8 = forward(last, state, True)
        for n, (layer, chunk) in enumerate(((0, 5), (0, 6), (1, 0), (1, 1), (1, 3))):
            pl.when(h == n)(lambda: poll(layer, chunk))
        m = jnp.max(m8, axis=0, keepdims=True)
        f = jnp.exp2((m8 - m) * LOG2)
        inverse = 1.0 / jnp.sum(total8 * f, axis=0, keepdims=True)
        delta = jnp.sum(weighted8 * f, axis=0, keepdims=True) * inverse

        def backward(b, dq):
            probs = []
            mixed = []
            for n in range(PARTS):
                rows = pl.ds(n * SUB, SUB)
                f = jnp.exp2((peaks[b, n] - m) * LOG2) * inverse
                p = (e_ref[b, rows].reshape(SUB // 8, 8, 256) * f[None]).reshape(SUB, 256)
                mixed.append((p * (d_ref[b, rows] - delta)).astype(BF))
                probs.append(p.astype(BF))
            probs = jnp.concatenate(probs, 0)
            mixed = jnp.concatenate(mixed, 0)
            here = pl.ds(4 * b, 4)
            shape = (4, 2, 2, 128, 128)
            dkv[1, here] += dot(probs, cotangent).reshape(shape)
            dkv[0, here] += dot(mixed, query).reshape(shape)
            keys = jnp.concatenate([kt[4 * b + n // 4, n % 4] for n in range(PARTS)], axis=1)
            return dq + dot(keys, mixed)

        dq = lax.fori_loop(0, last + 1, backward, jnp.zeros((128, 256), F32))
        for u in range(2):
            a_all[2 * h + u, yl, yh] = (dq[:, u * 128 : (u + 1) * 128].T * SCALE).astype(BF)
        for t in range(3):
            a_send(h, t).start()
        for n, (layer, chunk) in ((3, (1, 2)), (4, (1, 4))):
            pl.when(h == n)(lambda: poll(layer, chunk))
        pl.when(h == 3)(first_layer)
        return carry

    lax.fori_loop(0, PAIRS, pair, 0)

    def s_send(zz):
        return send(sb.at[:, zz], sbr.at[:, zz], s_s.at[zz], s_r.at[zz], sibling)

    def y_send(zz):
        return send(yb.at[:, zz], ybr.at[:, zz], y_s.at[zz], y_r.at[zz], y_peers[0])

    def stage_sibling(zz, carry):
        sb[0, zz] = (dkv[0, zz, :, 1 - c] * SCALE).astype(BF)
        sb[1, zz] = dkv[1, zz, :, 1 - c].astype(BF)
        s_send(zz).start()
        return carry


    def stage_y(zz, carry):
        s_send(zz).wait_recv()
        for n, scale in ((0, SCALE), (1, 1.0)):
            far = dkv[n, zz, 1 - yh, c] * scale + sbr[n, zz, 1 - yh].astype(F32)
            yb[n, zz] = far.astype(BF)
        y_send(zz).start()
        for n, scale in ((0, SCALE), (1, 1.0)):
            dkv[n, zz, yh, c] = dkv[n, zz, yh, c] * scale + sbr[n, zz, yh].astype(F32)
        return carry

    def stage_z(zz, carry):
        y_send(zz).wait_recv()
        for n in range(2):
            near = dkv[n, zz, yh, c] + ybr[n, zz].astype(F32)
            dkv[n, zz, yh, c] = near
            zb[n, zz] = near.astype(BF)

        @pl.when(zz < z)
        def _():
            send(
                zb.at[:, zz], zr.at[:, z], z_s.at[zz], z_r.at[z], {"ctx": zz * 4 + r, "kvh": j}
            ).start()

        return carry

    def stage_both(zz, carry):
        stage_sibling(zz, carry)
        pl.when(zz > 1)(lambda: stage_y(zz - 2, None))
        return carry

    lax.fori_loop(0, z + 1, stage_both, 0)
    lax.fori_loop(jnp.maximum(z - 1, 0), z + 1, stage_y, 0)

    def finish(layer):
        ref = xr.at[:, layer]
        send(ref, ref, x_s.at[0], x_r.at[layer], sibling).wait_recv()
        total = ct[layer, :, x].astype(F32)
        for t in range(3):
            total = total + xr[t, layer].astype(F32)
        total = total.astype(BF)
        for half in range(2):
            fs[half, :, layer] = total[..., half * 128 : (half + 1) * 128]
        for t in range(3):
            f_send(layer, t).start()
        fr[layer, yh, :, yl] = fs[yh, yl, layer]

    def f_send(layer, t):
        ph, pw = y_places[t]
        return send(
            fs.at[ph, pw, layer], fr.at[layer, yh, :, yl], f_s.at[layer, t], f_r.at[layer, t], y_peers[t]
        )

    wait_rows(1)
    wait_weights(1, w_all.at[0, :, pl.ds(0, 5), 0])
    second_layer([z, shift(0, 1), shift(1, 1), shift(0, 2), shift(1, 2)])
    early = jnp.minimum(z + 1, 2)
    lax.fori_loop(0, early, stage_z, 0)
    poll(1, 5)
    poll(1, 6)
    wait_weights(2, w_all.at[0, :, pl.ds(0, 3), 0])
    second_layer([shift(0, 3), shift(1, 3), shift(0, 4)])
    finish(0)

    middle = jnp.minimum(z + 1, 6)
    lax.fori_loop(early, middle, stage_z, 0)
    finish(1)
    lax.fori_loop(middle, z + 1, stage_z, 0)

    def result(layer):
        for t in range(3):
            f_send(layer, t).wait_recv()
        turned_ref[layer] = fr[layer].reshape(640, 128)

    result(0)

    def gather_z(zz, carry):
        send(zb.at[:, z], zr.at[:, zz], z_s.at[z], z_r.at[zz], sides[0]).wait_recv()
        for n in range(2):
            dkv[n, z, yh, c] += zr[n, zz].astype(F32)
        return carry

    lax.fori_loop(z + 1, 8, gather_z, 0)
    for n in range(2):
        both_ref[n] = dkv[n, z, yh, c].astype(BF)
    result(1)

    for sem, ref in (
        (kv_s.at[0], kv.at[0, pl.ds(0, 7), :, 0]),
        (ky_s.at[0], kv.at[0, :, :, 0]),
        (kc_s.at[0], kv.at[0]),
        (w_s.at[0], w_all.at[:, :, pl.ds(0, 7), 0]),
        (wc_s.at[0], w_all.at[:, :, :, 0]),
        (ws_s.at[0], w_all.at[:, 0, 0, 0]),
        (x_s.at[0], xr),
        (a_s.at[0], a_all.at[:, 0, 0]),
        (a_s.at[1], a_all.at[:, 0, 0]),
        (a_s.at[2], a_all.at[:, 0, 0]),
    ):
        send(ref, ref, sem, kc_r.at[0], sibling).wait_send()
    for layer in range(2):
        for t in range(3):
            f_send(layer, t).wait_send()

    def drain(zz, carry):
        s_send(zz).wait_send()
        y_send(zz).wait_send()

        @pl.when(zz < z)
        def _():
            send(zb.at[:, zz], zr.at[:, z], z_s.at[zz], z_r.at[z], sides[0]).wait_send()

        return carry

    lax.fori_loop(0, z + 1, drain, 0)


def outputs_kernel(turned_ref, both_ref, out_ref, gk_ref, gv_ref):
    for layer in range(2):
        out_ref[layer] = turned_ref[layer].astype(F32).T.astype(BF)
    gk_ref[...] = both_ref[0]
    gv_ref[...] = both_ref[1]


def body(queries, keys, values, grad_out, query_weight):
    dma = pltpu.SemaphoreType.DMA
    vmem = pltpu.VMEM
    turned, both = pl.pallas_call(
        kernel,
        out_shape=(jax.ShapeDtypeStruct((2, 640, 128), BF), jax.ShapeDtypeStruct((2, 128, 128), BF)),
        in_specs=[pl.BlockSpec(memory_space=pl.ANY)] * 5,
        out_specs=[pl.BlockSpec(memory_space=pltpu.VMEM)] * 2,
        scratch_shapes=[
            vmem((2, 8, 2, 2, 128, 128), BF),
            vmem((8, 4, 128, 128), BF),
            vmem((2, BLOCK, 256), F32),
            vmem((2, BLOCK, 256), F32),
            vmem((2, PARTS, 8, 256), F32),
            vmem((10, 128, 128), BF),
            vmem((10, 128, 128), BF),
            vmem((2, 8, 2, 2, 128, 128), F32),
            vmem((2, 2, 8, 2, 80, 640), BF),
            vmem((10, 2, 2, 128, 128), BF),
            vmem((2, 2, 4, 2, 80, 256), BF),
            vmem((3, 2, 2, 2, 80, 256), BF),
            vmem((2, 2, 2, 2, 80, 128), BF),
            vmem((2, 2, 2, 2, 80, 128), BF),
            vmem((2, 8, 2, 128, 128), BF),
            vmem((2, 8, 2, 128, 128), BF),
            vmem((2, 8, 128, 128), BF),
            vmem((2, 8, 128, 128), BF),
            vmem((2, 8, 128, 128), BF),
            vmem((2, 8, 128, 128), BF),
            dma((1,)), dma((2, 7)), dma((1,)), dma((16,)), dma((1,)), dma((1,)),
            dma((1,)), dma((2,)), dma((1,)), dma((2, 2, 7)), dma((1,)), dma((3,)),
            dma((3,)), dma((2, 3)), dma((1,)), dma((2,)), dma((2, 3)), dma((2, 3)),
            dma((8,)), dma((8,)), dma((8,)), dma((8,)), dma((8,)), dma((8,)), dma((5,)),
        ],
        compiler_params=pltpu.CompilerParams(
            collective_id=0, has_side_effects=True, vmem_limit_bytes=56 << 20
        ),
    )(queries, keys, values, grad_out, query_weight)
    return pl.pallas_call(
        outputs_kernel,
        out_shape=(
            jax.ShapeDtypeStruct((2, 128, 640), BF),
            jax.ShapeDtypeStruct((128, 128), BF),
            jax.ShapeDtypeStruct((128, 128), BF),
        ),
        in_specs=[pl.BlockSpec(memory_space=pltpu.VMEM)] * 2,
        out_specs=[pl.BlockSpec(memory_space=pltpu.VMEM)] * 3,
    )(turned, both)


def solution(mesh):
    cols = P(None, "ctx", "kvh")
    flat = P("ctx", "kvh")
    return jax.shard_map(
        body,
        mesh=mesh,
        in_specs=(cols, flat, flat, cols, cols),
        out_specs=(cols, flat, flat),
        check_vma=False,
    )
```

```python
import jax
import jax.numpy as jnp
from jax import lax
from jax.experimental import pallas as pl
from jax.experimental.pallas import tpu as pltpu
from jax.sharding import PartitionSpec as P

SCALE = 128 ** -0.5
LOG2 = SCALE * 1.4426950408889634
LOWEST = -1e30
NT = (((1,), (1,)), ((), ()))
MESH = pl.DeviceIdType.MESH
BF = jnp.bfloat16
F32 = jnp.float32
BLOCK = 2048
SUB = 128
PARTS = BLOCK // SUB
PAIRS = 5


def dot_nt(a, b):
    return lax.dot_general(a, b, NT, preferred_element_type=F32)


def dot(a, b):
    return jnp.dot(a, b, preferred_element_type=F32)


def send(src, dst, send_sem, recv_sem, device):
    return pltpu.make_async_remote_copy(
        src_ref=src,
        dst_ref=dst,
        send_sem=send_sem,
        recv_sem=recv_sem,
        device_id=device,
        device_id_type=MESH,
    )


def kernel(
    q_ref, k_ref, v_ref, do_ref, w_ref,
    turned_ref, both_ref,
    kv, kt, e_ref, d_ref, peaks, qs, dos, dkv, w_all, a_all, ct, xr, fs, fr,
    sb, sbr, yb, ybr, zb, zr,
    kv_s, kv_r, ky_s, ky_r, kc_s, kc_r,
    ws_s, ws_r, w_s, w_r, wc_s, wc_r,
    a_s, a_r, x_s, x_r, f_s, f_r,
    s_s, s_r, y_s, y_r, z_s, z_r, in_s,
):
    i = lax.axis_index("ctx")
    j = lax.axis_index("kvh")
    z = lax.div(i, 4)
    r = lax.rem(i, 4)
    yh = lax.div(r, 2)
    c = lax.rem(i, 2)
    yl = lax.div(j, 4)
    x = lax.rem(j, 4)

    def ring(a):
        return lax.rem(a + 8, 8)

    sibling = {"ctx": i + 1 - 2 * c, "kvh": j}
    sides = [{"ctx": ring(z + 1) * 4 + r, "kvh": j}, {"ctx": ring(z - 1) * 4 + r, "kvh": j}]
    flip_i = i + 2 - 4 * yh
    flip_j = j + 4 - 8 * yl
    y_peers = [{"ctx": flip_i, "kvh": j}, {"ctx": i, "kvh": flip_j}, {"ctx": flip_i, "kvh": flip_j}]
    y_places = [(1 - yh, yl), (yh, 1 - yl), (1 - yh, 1 - yl)]
    x_places = [lax.rem(x + t, 4) for t in (1, 2, 3)]
    x_peers = [{"ctx": i, "kvh": yl * 4 + p} for p in x_places]

    barrier = pltpu.get_barrier_semaphore()
    for peer in [sibling] + y_peers + x_peers:
        pl.semaphore_signal(barrier, inc=1, device_id=peer, device_id_type=MESH)
    for t in range(1, 8):
        pl.semaphore_signal(
            barrier, inc=1, device_id={"ctx": ring(z + t) * 4 + r, "kvh": j}, device_id_type=MESH
        )

    loads = [
        pltpu.make_async_copy(k_ref, kv.at[0, z, yh, c], in_s.at[0]),
        pltpu.make_async_copy(v_ref, kv.at[1, z, yh, c], in_s.at[1]),
        pltpu.make_async_copy(
            w_ref.at[:, pl.ds(pl.multiple_of(yl * 80, 16), 80), :], w_all.at[:, yl, z, c], in_s.at[2]
        ),
    ]
    for load in loads:
        load.start()
    for layer in range(2):
        for h in range(PAIRS):
            column = pl.ds(h * 128, 128)
            g = layer * PAIRS + h
            pltpu.make_async_copy(q_ref.at[layer, :, column], qs.at[g], in_s.at[3]).start()
            pltpu.make_async_copy(do_ref.at[layer, :, column], dos.at[g], in_s.at[4]).start()
    dkv[...] = jnp.zeros_like(dkv)
    for load in loads:
        load.wait()
    pl.semaphore_wait(barrier, 14)

    def shift(way, d):
        return ring(z - d) if way == 0 else ring(z + d)

    reach = [2, 2, 1, 1, 3, 3, 4]

    def kv_arrival(way, n):
        return (way + n) % 2, ring(z - reach[n]) if way == 0 else ring(z + reach[n])

    def kv_hop(way, n):
        if n < 4:
            part, zz = (way + n) % 2, z
        else:
            part, zz = kv_arrival(way, n - 4 if n < 6 else 0)
        ref = kv.at[part, zz, yh, c]
        jump = 2 if n in (0, 1, 6) else 1
        target = {"ctx": (ring(z + jump) if way == 0 else ring(z - jump)) * 4 + r, "kvh": j}
        return send(ref, ref, kv_s.at[0], kv_r.at[way, n], target)

    def kv_wait(way, n):
        part, zz = kv_arrival(way, n)
        ref = kv.at[part, zz, yh, c]
        send(ref, ref, kv_s.at[0], kv_r.at[way, n], sides[way]).wait_recv()

    def kv_y(n, part, zz, place):
        ref = kv.at[part, zz, place, c]
        return send(ref, ref, ky_s.at[0], ky_r.at[n], y_peers[0])

    def kv_c(part, zz, place):
        ref = kv.at[part, zz, place, c]
        return send(ref, ref, kc_s.at[0], kc_r.at[0], sibling)

    def flip_key(zz, place, core):
        kt[zz, 2 * place + core] = kv[0, zz, place, core].astype(F32).T.astype(BF)

    def w_half(layer, way, n):
        if layer == 0:
            return lax.rem(yl + (1 if way == 1 and n == 6 else n % 2), 2)
        return lax.rem(yl + way + n, 2)

    def w_ref_of(layer, way, n, zz):
        return w_all.at[layer, w_half(layer, way, n), zz, c]

    def w_send(layer, way, n):
        ref = w_ref_of(layer, way, n, z if n < 2 else shift(way, n // 2))
        return send(ref, ref, w_s.at[0], w_r.at[layer, way, n], sides[way])

    def w_sib(ref, group):
        return send(ref, ref, wc_s.at[0], wc_r.at[group], sibling)

    def own_weight(layer, n):
        for way in range(2):
            w_send(layer, way, n).start()
        w_sib(w_ref_of(layer, 0, n, z), layer).start()

    def poll(layer, n):
        for way in range(2):
            ref = w_ref_of(layer, way, n, shift(way, n // 2 + 1))
            send(ref, ref, w_s.at[0], w_r.at[layer, way, n], sides[way]).wait_recv()
            last_from = 5 if layer == 0 and way == 1 else 4
            if n < 4 or n == last_from:
                w_send(layer, way, 6 if n == last_from else n + 2).start()
            w_sib(ref, 2 if layer == 1 and n > 3 else layer).start()
        if layer == 0 and n in (3, 4):
            own_weight(1, n - 3)

    def w_swap(layer):
        return send(
            w_ref.at[layer, pl.ds(pl.multiple_of((1 - yl) * 80, 16), 80), :],
            w_all.at[layer, yl, z, c],
            ws_s.at[0],
            ws_r.at[layer],
            y_peers[1],
        )

    for n in range(4):
        for way in range(2):
            kv_hop(way, n).start()
    for n in range(2):
        kv_y(n, n, z, yh).start()
        kv_c(n, z, yh).start()
    w_swap(0).start()
    own_weight(0, 0)
    flip_key(z, yh, c)

    def pieces(n):
        if n < 0:
            return [(0, 0, z), (1, 1, z)]
        return [(2 + 2 * n + way,) + kv_arrival(way, n) for way in range(2)]

    def relay(n):
        for m, part, zz in pieces(n):
            kv_y(m, part, zz, 1 - yh).wait_recv()
            kv_c(part, zz, 1 - yh).start()
        for m, part, zz in pieces(n):
            if part == 0:
                if n >= 0:
                    flip_key(zz, yh, c)
                flip_key(zz, 1 - yh, c)

    def arrive(n):
        for way in range(2):
            kv_wait(way, n)
            if n == 0:
                kv_hop(way, 6).start()
            if n < 2:
                kv_hop(way, n + 4).start()
            part, zz = kv_arrival(way, n)
            kv_y(2 + 2 * n + way, part, zz, yh).start()
            kv_c(part, zz, yh).start()

    arrive(0)
    arrive(1)
    relay(-1)
    arrive(2)
    arrive(3)
    w_swap(0).wait_recv()
    own_weight(0, 1)
    relay(0)
    poll(0, 0)
    relay(1)
    arrive(4)
    arrive(5)
    arrive(6)
    relay(2)
    poll(0, 1)
    w_swap(1).start()
    relay(3)
    poll(0, 2)
    relay(4)
    w_swap(1).wait_recv()
    poll(0, 3)
    relay(5)
    relay(6)
    poll(0, 4)
    others = kv.at[:, :, :, 1 - c]
    send(others, others, kc_s.at[0], kc_r.at[0], sibling).wait_recv()
    for zz in range(8):
        for spot in range(2):
            flip_key(zz, spot, 1 - c)

    pltpu.make_async_copy(qs, qs, in_s.at[3]).wait()
    pltpu.make_async_copy(dos, dos, in_s.at[4]).wait()
    last = lax.div(z, 4)
    lane = lax.broadcasted_iota(jnp.int32, (SUB, 256), 1)
    place = z * 512 + r * 128 + lax.rem(lane, 128)

    def a_send(h, t):
        ref = a_all.at[pl.ds(2 * h, 2), yl, yh]
        return send(ref, ref, a_s.at[t], a_r.at[lax.div(h, 3), t], y_peers[t])

    def x_send(layer, t):
        return send(ct.at[layer, :, x_places[t]], xr.at[t, layer], x_s.at[0], x_r.at[layer], x_peers[t])

    def wait_rows(layer):
        part = pl.ds(0, 6) if layer == 0 else pl.ds(6, 4)
        for t, (ph, pw) in enumerate(y_places):
            ref = a_all.at[part, pw, ph]
            send(ref, ref, a_s.at[t], a_r.at[layer, t], y_peers[t]).wait_recv()

    def wait_weights(group, ref):
        send(ref, ref, wc_s.at[0], wc_r.at[group], sibling).wait_recv()

    def gathered(layer, w):
        return jnp.concatenate([a_all[layer * PAIRS + h, w].reshape(256, 128) for h in range(PAIRS)], axis=1)

    def first_layer():
        wait_rows(0)
        wait_weights(0, w_all.at[0, :, :, 1 - c])
        rows = [gathered(0, w) for w in range(2)]
        for hi in range(2):
            total = dot_nt(w_all[0, 0, 4 * hi : 4 * hi + 4].reshape(640, 640), rows[0])
            total = total + dot_nt(w_all[0, 1, 4 * hi : 4 * hi + 4].reshape(640, 640), rows[1])
            ct[0, hi] = total.astype(BF).reshape(4, 2, 80, 256)
        for t in range(3):
            x_send(0, t).start()

    def second_layer(planes):
        rows = [gathered(1, w) for w in range(2)]
        for zz in planes:
            total = dot_nt(w_all[1, 0, zz].reshape(160, 640), rows[0])
            total = total + dot_nt(w_all[1, 1, zz].reshape(160, 640), rows[1])
            hi = lax.div(zz, 4)
            p = lax.rem(zz, 4)
            ct[1, hi, p] = total.astype(BF).reshape(2, 80, 256)
            t = lax.rem(p - x + 4, 4)

            @pl.when(t > 0)
            def _():
                send(
                    ct.at[1, hi, p],
                    xr.at[t - 1, 1, hi],
                    x_s.at[0],
                    x_r.at[1],
                    {"ctx": i, "kvh": yl * 4 + p},
                ).start()

    def pair(h, carry):
        two = pl.ds(2 * h, 2)
        query = qs[two].reshape(256, 128)
        cotangent = dos[two].reshape(256, 128)

        def forward(b, state, masked=False):
            m, total, weighted = state
            for n in range(PARTS):
                rows = pl.ds(n * SUB, SUB)
                zz = 4 * b + n // 4
                s = dot_nt(kv[0, zz, n // 2 % 2, n % 2], query)
                if masked:
                    key_place = lax.broadcasted_iota(jnp.int32, (SUB, 256), 0) + (b * BLOCK + n * SUB)
                    s = jnp.where(key_place <= place, s, LOWEST)
                d = dot_nt(kv[1, zz, n // 2 % 2, n % 2], cotangent)
                s = s.reshape(SUB // 8, 8, 256)
                peak = jnp.max(s, axis=0)
                e = jnp.exp2((s - peak[None]) * LOG2)
                part_total = jnp.sum(e, axis=0)
                part_weighted = jnp.sum(e * d.reshape(SUB // 8, 8, 256), axis=0)
                e_ref[b, rows] = e.reshape(SUB, 256)
                d_ref[b, rows] = d
                peaks[b, n] = peak
                new = jnp.maximum(m, peak)
                f0 = jnp.exp2((m - new) * LOG2)
                f1 = jnp.exp2((peak - new) * LOG2)
                total = total * f0 + part_total * f1
                weighted = weighted * f0 + part_weighted * f1
                m = new
            return m, total, weighted

        zero = jnp.zeros((8, 256), F32)
        state = lax.fori_loop(0, last, forward, (jnp.full((8, 256), LOWEST, F32), zero, zero))
        m8, total8, weighted8 = forward(last, state, True)
        for n, (layer, chunk) in enumerate(((0, 5), (0, 6), (1, 0), (1, 1), (1, 3))):
            pl.when(h == n)(lambda: poll(layer, chunk))
        m = jnp.max(m8, axis=0, keepdims=True)
        f = jnp.exp2((m8 - m) * LOG2)
        inverse = 1.0 / jnp.sum(total8 * f, axis=0, keepdims=True)
        delta = jnp.sum(weighted8 * f, axis=0, keepdims=True) * inverse

        def backward(b, dq):
            probs = []
            mixed = []
            for n in range(PARTS):
                rows = pl.ds(n * SUB, SUB)
                f = jnp.exp2((peaks[b, n] - m) * LOG2) * inverse
                p = (e_ref[b, rows].reshape(SUB // 8, 8, 256) * f[None]).reshape(SUB, 256)
                mixed.append((p * (d_ref[b, rows] - delta)).astype(BF))
                probs.append(p.astype(BF))
            probs = jnp.concatenate(probs, 0)
            mixed = jnp.concatenate(mixed, 0)
            here = pl.ds(4 * b, 4)
            shape = (4, 2, 2, 128, 128)
            dkv[1, here] += dot(probs, cotangent).reshape(shape)
            dkv[0, here] += dot(mixed, query).reshape(shape)
            keys = jnp.concatenate([kt[4 * b + n // 4, n % 4] for n in range(PARTS)], axis=1)
            return dq + dot(keys, mixed)

        dq = lax.fori_loop(0, last + 1, backward, jnp.zeros((128, 256), F32))
        for u in range(2):
            a_all[2 * h + u, yl, yh] = (dq[:, u * 128 : (u + 1) * 128].T * SCALE).astype(BF)
        for t in range(3):
            a_send(h, t).start()
        for n, (layer, chunk) in ((3, (1, 2)), (4, (1, 4))):
            pl.when(h == n)(lambda: poll(layer, chunk))
        pl.when(h == 3)(first_layer)
        return carry

    lax.fori_loop(0, PAIRS, pair, 0)

    def s_send(zz):
        return send(sb.at[:, zz], sbr.at[:, zz], s_s.at[zz], s_r.at[zz], sibling)

    def y_send(zz):
        return send(yb.at[:, zz], ybr.at[:, zz], y_s.at[zz], y_r.at[zz], y_peers[0])

    def stage_sibling(zz, carry):
        sb[0, zz] = (dkv[0, zz, :, 1 - c] * SCALE).astype(BF)
        sb[1, zz] = dkv[1, zz, :, 1 - c].astype(BF)
        s_send(zz).start()
        return carry


    def stage_y(zz, carry):
        s_send(zz).wait_recv()
        for n, scale in ((0, SCALE), (1, 1.0)):
            far = dkv[n, zz, 1 - yh, c] * scale + sbr[n, zz, 1 - yh].astype(F32)
            yb[n, zz] = far.astype(BF)
        y_send(zz).start()
        for n, scale in ((0, SCALE), (1, 1.0)):
            dkv[n, zz, yh, c] = dkv[n, zz, yh, c] * scale + sbr[n, zz, yh].astype(F32)
        return carry

    def stage_z(zz, carry):
        y_send(zz).wait_recv()
        for n in range(2):
            near = dkv[n, zz, yh, c] + ybr[n, zz].astype(F32)
            dkv[n, zz, yh, c] = near
            zb[n, zz] = near.astype(BF)

        @pl.when(zz < z)
        def _():
            send(
                zb.at[:, zz], zr.at[:, z], z_s.at[zz], z_r.at[z], {"ctx": zz * 4 + r, "kvh": j}
            ).start()

        return carry

    def stage_both(zz, carry):
        stage_sibling(zz, carry)
        pl.when(zz > 1)(lambda: stage_y(zz - 2, None))
        return carry

    lax.fori_loop(0, z + 1, stage_both, 0)
    lax.fori_loop(jnp.maximum(z - 1, 0), z + 1, stage_y, 0)

    def finish(layer):
        ref = xr.at[:, layer]
        send(ref, ref, x_s.at[0], x_r.at[layer], sibling).wait_recv()
        total = ct[layer, :, x].astype(F32)
        for t in range(3):
            total = total + xr[t, layer].astype(F32)
        total = total.astype(BF)
        for half in range(2):
            fs[half, :, layer] = total[..., half * 128 : (half + 1) * 128]
        for t in range(3):
            f_send(layer, t).start()
        fr[layer, yh, :, yl] = fs[yh, yl, layer]

    def f_send(layer, t):
        ph, pw = y_places[t]
        return send(
            fs.at[ph, pw, layer], fr.at[layer, yh, :, yl], f_s.at[layer, t], f_r.at[layer, t], y_peers[t]
        )

    wait_rows(1)
    wait_weights(1, w_all.at[0, :, pl.ds(0, 5), 0])
    second_layer([z, shift(0, 1), shift(1, 1), shift(0, 2), shift(1, 2)])
    finish(0)
    early = jnp.minimum(z + 1, 2)
    lax.fori_loop(0, early, stage_z, 0)
    poll(1, 5)
    poll(1, 6)
    wait_weights(2, w_all.at[0, :, pl.ds(0, 3), 0])
    second_layer([shift(0, 3), shift(1, 3), shift(0, 4)])

    middle = jnp.minimum(z + 1, 6)
    lax.fori_loop(early, middle, stage_z, 0)
    finish(1)
    lax.fori_loop(middle, z + 1, stage_z, 0)

    def result(layer):
        for t in range(3):
            f_send(layer, t).wait_recv()
        turned_ref[layer] = fr[layer].reshape(640, 128)

    result(0)

    def gather_z(zz, carry):
        send(zb.at[:, z], zr.at[:, zz], z_s.at[z], z_r.at[zz], sides[0]).wait_recv()
        for n in range(2):
            dkv[n, z, yh, c] += zr[n, zz].astype(F32)
        return carry

    lax.fori_loop(z + 1, 8, gather_z, 0)
    for n in range(2):
        both_ref[n] = dkv[n, z, yh, c].astype(BF)
    result(1)

    for sem, ref in (
        (kv_s.at[0], kv.at[0, pl.ds(0, 7), :, 0]),
        (ky_s.at[0], kv.at[0, :, :, 0]),
        (kc_s.at[0], kv.at[0]),
        (w_s.at[0], w_all.at[:, :, pl.ds(0, 7), 0]),
        (wc_s.at[0], w_all.at[:, :, :, 0]),
        (ws_s.at[0], w_all.at[:, 0, 0, 0]),
        (x_s.at[0], xr),
        (a_s.at[0], a_all.at[:, 0, 0]),
        (a_s.at[1], a_all.at[:, 0, 0]),
        (a_s.at[2], a_all.at[:, 0, 0]),
    ):
        send(ref, ref, sem, kc_r.at[0], sibling).wait_send()
    for layer in range(2):
        for t in range(3):
            f_send(layer, t).wait_send()

    def drain(zz, carry):
        s_send(zz).wait_send()
        y_send(zz).wait_send()

        @pl.when(zz < z)
        def _():
            send(zb.at[:, zz], zr.at[:, z], z_s.at[zz], z_r.at[z], sides[0]).wait_send()

        return carry

    lax.fori_loop(0, z + 1, drain, 0)


def outputs_kernel(turned_ref, both_ref, out_ref, gk_ref, gv_ref):
    for layer in range(2):
        out_ref[layer] = turned_ref[layer].astype(F32).T.astype(BF)
    gk_ref[...] = both_ref[0]
    gv_ref[...] = both_ref[1]


def body(queries, keys, values, grad_out, query_weight):
    dma = pltpu.SemaphoreType.DMA
    vmem = pltpu.VMEM
    turned, both = pl.pallas_call(
        kernel,
        out_shape=(jax.ShapeDtypeStruct((2, 640, 128), BF), jax.ShapeDtypeStruct((2, 128, 128), BF)),
        in_specs=[pl.BlockSpec(memory_space=pl.ANY)] * 5,
        out_specs=[pl.BlockSpec(memory_space=pltpu.VMEM)] * 2,
        scratch_shapes=[
            vmem((2, 8, 2, 2, 128, 128), BF),
            vmem((8, 4, 128, 128), BF),
            vmem((2, BLOCK, 256), F32),
            vmem((2, BLOCK, 256), F32),
            vmem((2, PARTS, 8, 256), F32),
            vmem((10, 128, 128), BF),
            vmem((10, 128, 128), BF),
            vmem((2, 8, 2, 2, 128, 128), F32),
            vmem((2, 2, 8, 2, 80, 640), BF),
            vmem((10, 2, 2, 128, 128), BF),
            vmem((2, 2, 4, 2, 80, 256), BF),
            vmem((3, 2, 2, 2, 80, 256), BF),
            vmem((2, 2, 2, 2, 80, 128), BF),
            vmem((2, 2, 2, 2, 80, 128), BF),
            vmem((2, 8, 2, 128, 128), BF),
            vmem((2, 8, 2, 128, 128), BF),
            vmem((2, 8, 128, 128), BF),
            vmem((2, 8, 128, 128), BF),
            vmem((2, 8, 128, 128), BF),
            vmem((2, 8, 128, 128), BF),
            dma((1,)), dma((2, 7)), dma((1,)), dma((16,)), dma((1,)), dma((1,)),
            dma((1,)), dma((2,)), dma((1,)), dma((2, 2, 7)), dma((1,)), dma((3,)),
            dma((3,)), dma((2, 3)), dma((1,)), dma((2,)), dma((2, 3)), dma((2, 3)),
            dma((8,)), dma((8,)), dma((8,)), dma((8,)), dma((8,)), dma((8,)), dma((5,)),
        ],
        compiler_params=pltpu.CompilerParams(
            collective_id=0, has_side_effects=True, vmem_limit_bytes=56 << 20
        ),
    )(queries, keys, values, grad_out, query_weight)
    return pl.pallas_call(
        outputs_kernel,
        out_shape=(
            jax.ShapeDtypeStruct((2, 128, 640), BF),
            jax.ShapeDtypeStruct((128, 128), BF),
            jax.ShapeDtypeStruct((128, 128), BF),
        ),
        in_specs=[pl.BlockSpec(memory_space=pltpu.VMEM)] * 2,
        out_specs=[pl.BlockSpec(memory_space=pltpu.VMEM)] * 3,
    )(turned, both)


def solution(mesh):
    cols = P(None, "ctx", "kvh")
    flat = P("ctx", "kvh")
    return jax.shard_map(
        body,
        mesh=mesh,
        in_specs=(cols, flat, flat, cols, cols),
        out_specs=(cols, flat, flat),
        check_vma=False,
    )
```
